128 devices in a mesh: dp: 8 (over x, z_hi), tensor: 16 (over y, z_lo, core).
Axes of the slice: x: 4, y: 4, z: 4 (z_hi: 2, z_lo: 2; z = z_hi * 2 + z_lo), core: 2. Of those that a mesh axis runs over, the one named last changes fastest.
Arguments:
- tokens: bfloat16 [16384, 1024], P(('dp', 'tensor')), may hold values from -6 to 6
- w_qkv: bfloat16 [1024, 16, 192], P(None, 'tensor'), may hold values from -0.25 to 0.25
- b_qkv: bfloat16 [16, 192], P('tensor'), may hold values from -2 to 2
- w_out: bfloat16 [16, 64, 1024], P('tensor'), may hold values from -0.75 to 0.75
- w_up: bfloat16 [1024, 4096], P(None, 'tensor'), may hold values from -0.1875 to 0.1875
- b_up: bfloat16 [4096], P('tensor'), may hold values from -3 to 3
- w_down: bfloat16 [4096, 1024], P('tensor'), may hold values from -0.09375 to 0.09375
- out_bias: bfloat16 [1024], replicated, may hold values from -2 to 2
- ln1_gain: bfloat16 [1024], replicated, may hold values from 0.5 to 1.5
- ln1_shift: bfloat16 [1024], replicated, may hold values from -2 to 2
- ln2_gain: bfloat16 [1024], replicated, may hold values from 0.5 to 1.5
- ln2_shift: bfloat16 [1024], replicated, may hold values from -2 to 2
- cotangent: bfloat16 [16384, 1024], P(('dp', 'tensor')), may hold values from -6 to 6
Outputs:
- layer_out: bfloat16 [16384, 1024], P(('dp', 'tensor'))
- input_grad: bfloat16 [16384, 1024], P(('dp', 'tensor'))
- grad_w_qkv: float32 [1024, 16, 192], P(None, 'tensor')
- grad_b_qkv: float32 [16, 192], P('tensor')
- grad_w_out: float32 [16, 64, 1024], P('tensor')
- grad_w_up: float32 [1024, 4096], P(None, 'tensor')
- grad_b_up: float32 [4096], P('tensor')
- grad_w_down: float32 [4096, 1024], P('tensor')
- grad_out_bias: float32 [1024], replicated
- grad_ln1_gain: float32 [1024], replicated
- grad_ln1_shift: float32 [1024], replicated
- grad_ln2_gain: float32 [1024], replicated
- grad_ln2_shift: float32 [1024], replicated
The draws below stay inside these ranges and needn't reach their ends.
All inputs are finite; a program needn't handle non-finite values.
Results may differ from the reference program's by a relative error of at most 0.019.
The reference program's roundings to bfloat16 on the way count: a program that leaves them out, or rounds other values in their place, can miss the bound.
Values may be sent and summed in bfloat16 or wider, within the bound.
No kernel may reach another device: no remote copies, remote signals or barrier semaphores. Data moves between devices by JAX's collectives and lax.ppermute only.
A program may use at most 128 MiB of HBM per device.

```python
import jax
import jax.numpy as jnp
from jax import lax

D = 1024
HEADS = 16
HEAD = 64
ROT = 16
FF = 4096
LEN = 2048
SEQS = 1
TOKENS = 16384
N_DP = 8


def shard_levels(rng, dims, pieces, low, largest):
    level = 1.0
    for axis_at, blocks in pieces:
        steps = jax.random.uniform(jax.random.fold_in(jax.random.fold_in(rng, 6), axis_at), (blocks,), jnp.float32, low / len(pieces), largest / len(pieces))
        level = level * jnp.repeat(jnp.exp(steps), dims[axis_at] // blocks).reshape((-1,) + (1,) * (len(dims) - 1 - axis_at))
    return level


def bell_draw(rng, extent, spread, reach, shards=(), kind=jnp.bfloat16):
    array = jax.random.normal(rng, extent, jnp.float32) * spread
    if len(shards) > 0:
        array = shard_levels(rng, extent, shards, -0.22, 0.18) * array
    return jnp.clip(array, min=-reach, max=reach).astype(kind)


def setup_inputs(seed: int = 0) -> dict:
    arg_keys = jax.random.split(jax.random.key(seed), 14)
    return {
        "tokens": bell_draw(arg_keys[0], (TOKENS, D), 1.0, 6.0, ((0, 128),)),
        "w_qkv": bell_draw(arg_keys[1], (D, HEADS, 3 * HEAD), (D // 2) ** -0.5, 0.25, ((1, 16),)),
        "b_qkv": bell_draw(arg_keys[2], (HEADS, 3 * HEAD), 0.3, 2.0, ((0, 16),)),
        "w_out": bell_draw(arg_keys[3], (HEADS, HEAD, D), (D // 16) ** -0.5, 0.75, ((0, 16),)),
        "w_up": bell_draw(arg_keys[4], (D, FF), D ** -0.5, 0.1875, ((1, 16),)),
        "b_up": bell_draw(arg_keys[5], (FF,), 0.5, 3.0, ((0, 16),)),
        "w_down": bell_draw(arg_keys[6], (FF, D), FF ** -0.5, 0.09375, ((0, 16),)),
        "out_bias": bell_draw(arg_keys[7], (D,), 0.3, 2.0),
        "ln1_gain": jnp.clip(1.0 + 0.1 * jax.random.normal(arg_keys[8], (D,), jnp.float32), 0.5, 1.5).astype(jnp.bfloat16),
        "ln1_shift": bell_draw(arg_keys[9], (D,), 0.3, 2.0),
        "ln2_gain": jnp.clip(1.0 + 0.1 * jax.random.normal(arg_keys[10], (D,), jnp.float32), 0.5, 1.5).astype(jnp.bfloat16),
        "ln2_shift": bell_draw(arg_keys[11], (D,), 0.3, 2.0),
        "cotangent": bell_draw(arg_keys[12], (TOKENS, D), 1.0, 6.0, ((0, 128),)),
    }


@jax.custom_vjp
def low(v):
    return lax.optimization_barrier(v.astype(jnp.bfloat16)).astype(jnp.float32)

@jax.custom_vjp
def low_back(v):
    return v

def low_keep(v):
    return (low(v), None)

def low_pass(kept, grad):
    return (grad,)

def back_keep(v):
    return (v, None)

def back_low(kept, grad):
    return (low(grad),)
low.defvjp(low_keep, low_pass)
low_back.defvjp(back_keep, back_low)
EPS = 1e-05
HIGH = lax.Precision.HIGHEST

def layer_norm(values, gain, shift):
    center = values - lax.optimization_barrier(jnp.mean(values, axis=-1, keepdims=True))
    variance = lax.optimization_barrier(jnp.mean(center * center, axis=-1, keepdims=True))
    return center * lax.rsqrt(variance + EPS) * gain + shift

def rotary_tables(length, rotary):
    places = jnp.arange(length, dtype=jnp.float32)
    inverse = 10000.0 ** (-2.0 * jnp.arange(rotary // 2, dtype=jnp.float32) / rotary)
    angles = places[:, None] * inverse[None, :]
    return (jnp.cos(angles)[:, None, :], jnp.sin(angles)[:, None, :])

def rotate(values, cosine, sine, rotary):
    half = rotary // 2
    first = values[..., :half]
    second = values[..., half:rotary]
    return jnp.concatenate([first * cosine - second * sine, second * cosine + first * sine, values[..., rotary:]], axis=-1)

def attention(queries, keys_all, values_all):
    length = queries.shape[0]
    block = min(512, length)
    count = length // block
    scale = HEAD ** (-0.5)
    key_places = jnp.arange(length, dtype=jnp.int32)

    def one_block(index):
        start = index * block
        query_rows = lax.dynamic_slice_in_dim(queries, start, block, 0)
        scores = low_back(jnp.einsum('bhe,the->hbt', query_rows, keys_all, precision=HIGH) * scale)
        places = start + jnp.arange(block, dtype=jnp.int32)
        scores = jnp.where(places[:, None] >= key_places[None, :], scores, -1e+30)
        top = lax.optimization_barrier(jnp.max(scores, axis=-1, keepdims=True))
        expo = jnp.exp(scores - top)
        probs = expo / lax.optimization_barrier(jnp.sum(expo, axis=-1, keepdims=True))
        context = jnp.einsum('hbt,the->bhe', low(probs), values_all, precision=HIGH)
        return low(low_back(context))
    blocks = lax.map(jax.checkpoint(one_block), jnp.arange(count, dtype=jnp.int32))
    return blocks.reshape(length, queries.shape[1], queries.shape[2])

def sequence_forward(seq_rows, w_qkv, b_qkv, w_out, w_up, b_up, w_down, out_bias, gain_one, shift_one, gain_two, shift_two):
    normed_one = low(layer_norm(seq_rows, gain_one, shift_one))
    normed_two = low(layer_norm(seq_rows, gain_two, shift_two))
    projected = low_back(jnp.einsum('td,dhe->the', normed_one, w_qkv, precision=HIGH) + b_qkv)
    cosine, sine = rotary_tables(seq_rows.shape[0], ROT)
    queries = low(rotate(projected[..., :HEAD], cosine, sine, ROT))
    keys_all = low(rotate(projected[..., HEAD:2 * HEAD], cosine, sine, ROT))
    values_all = low(projected[..., 2 * HEAD:])
    context = attention(queries, keys_all, values_all)
    attended = jnp.einsum('the,hed->td', context, w_out, precision=HIGH)
    hidden = low_back(jnp.dot(normed_two, w_up, precision=HIGH) + b_up)
    activated = low(jax.nn.gelu(hidden, approximate=False))
    mixed = jnp.dot(activated, w_down, precision=HIGH)
    return seq_rows + attended + mixed + out_bias

def reference(tokens, w_qkv, b_qkv, w_out, w_up, b_up, w_down, out_bias, ln1_gain, ln1_shift, ln2_gain, ln2_shift, cotangent):
    params = tuple((item.astype(jnp.float32) for item in (w_qkv, b_qkv, w_out, w_up, b_up, w_down, out_bias, ln1_gain, ln1_shift, ln2_gain, ln2_shift)))
    seq_rows = tokens.astype(jnp.float32).reshape(SEQS * N_DP, LEN, D)
    seq_grads = cotangent.astype(jnp.float32).reshape(SEQS * N_DP, LEN, D)

    def one_sequence(totals, item):
        rows_here, grad_here = item
        result, pull = jax.vjp(sequence_forward, rows_here, *params)
        pulled = pull(grad_here)
        return (tuple((left + right for left, right in zip(totals, pulled[1:]))), (result, pulled[0]))
    zeros = tuple((jnp.zeros_like(item) for item in params))
    totals, (results, input_grads) = lax.scan(one_sequence, zeros, (seq_rows, seq_grads))
    layer_out = results.reshape(TOKENS, D).astype(jnp.bfloat16)
    input_grad = input_grads.reshape(TOKENS, D).astype(jnp.bfloat16)
    return (layer_out, input_grad, totals[0], totals[1], totals[2], totals[3], totals[4], totals[5], totals[6], totals[7], totals[8], totals[9], totals[10])
```

```python
from functools import partial

import jax
import jax.numpy as jnp
from jax import lax
from jax.sharding import PartitionSpec as P

ROT = 16
LEN = 2048


EPS = 1e-05


SAME_CORE = [[c + 2 * i for i in range(8)] for c in range(2)]
SAME_Z = [[c + 2 * i for i in range(4)] for c in range(2)]
PAIR = [(i, i ^ 1) for i in range(16)]
Z_PAIR = [(i, i ^ 1) for i in range(8)]


def swap_core(value):
    return lax.ppermute(value, "tensor", PAIR)


def trade_chips(blocks):
    return lax.all_to_all(blocks, "tensor", 0, 0, axis_index_groups=SAME_CORE, tiled=True)


def trade_x(blocks):
    return lax.all_to_all(blocks, "dp", 0, 0, axis_index_groups=SAME_Z, tiled=True)


def gather_rows(block):
    mine = trade_chips(jnp.broadcast_to(block[None], (8,) + block.shape))
    other = swap_core(mine)
    first_core = lax.axis_index("tensor") % 2 == 0
    even = jnp.where(first_core, mine, other)
    odd = jnp.where(first_core, other, mine)
    return jnp.stack([even, odd], axis=1).reshape(16 * block.shape[0], block.shape[1])


def scatter_rows(partial):
    core = lax.axis_index("tensor") % 2
    split = partial.reshape(8, 2, partial.shape[0] // 16, partial.shape[1])
    send = lax.dynamic_index_in_dim(split, 1 - core, 1, keepdims=False)
    keep = lax.dynamic_index_in_dim(split, core, 1, keepdims=False)
    other = swap_core(send)
    both = (keep.astype(jnp.float32) + other.astype(jnp.float32)).astype(jnp.bfloat16)
    return jnp.sum(trade_chips(both).astype(jnp.float32), axis=0)


def sum_dp(chunks):
    mine = jnp.sum(trade_x(chunks).astype(jnp.float32), axis=0)
    low = mine.astype(jnp.bfloat16)
    other = lax.ppermute(low, "dp", Z_PAIR)
    both = (low.astype(jnp.float32) + other.astype(jnp.float32)).astype(jnp.bfloat16)
    return trade_x(jnp.broadcast_to(both[None], chunks.shape)).astype(jnp.float32)


def sum_all(rows):
    chips = jnp.sum(trade_chips(jnp.broadcast_to(rows[None], (8,) + rows.shape)), axis=0)
    pair = chips + swap_core(chips)
    return jnp.sum(
        lax.all_to_all(jnp.broadcast_to(pair[None], (8,) + rows.shape), "dp", 0, 0, tiled=True),
        axis=0,
    )


def normalize(values):
    center = values - jnp.mean(values, axis=-1, keepdims=True)
    inverse = lax.rsqrt(jnp.mean(center * center, axis=-1, keepdims=True) + EPS)
    return (center * inverse, inverse)


def norm_back(scaled, normalized, inverse):
    centered = scaled - jnp.mean(scaled, axis=-1, keepdims=True)
    return inverse * (centered - normalized * jnp.mean(scaled * normalized, axis=-1, keepdims=True))


def rotary_tables(length, rotary):
    places = jnp.arange(length, dtype=jnp.float32)
    inverse = 10000.0 ** (-2.0 * jnp.arange(rotary // 2, dtype=jnp.float32) / rotary)
    angles = places[:, None] * inverse[None, :]
    return (jnp.cos(angles)[:, None, :], jnp.sin(angles)[:, None, :])


def rotate(values, cosine, sine, rotary):
    half = rotary // 2
    first = values[..., :half]
    second = values[..., half:rotary]
    return jnp.concatenate(
        [first * cosine - second * sine, second * cosine + first * sine, values[..., rotary:]],
        axis=-1,
    )


def block_scores(query_rows, keys_all, start, scale):
    block = query_rows.shape[0]
    scores = (
        jnp.einsum("bhe,the->hbt", query_rows, keys_all, preferred_element_type=jnp.float32) * scale
    )
    places = start + jnp.arange(block, dtype=jnp.int32)
    key_places = jnp.arange(keys_all.shape[0], dtype=jnp.int32)
    return jnp.where(places[:, None] >= key_places[None, :], scores, -1e30)


def attend_forward(queries, keys_all, values_all, scale):
    length = queries.shape[0]
    block = min(512, length)
    count = length // block

    def one_block(index):
        start = index * block
        query_rows = lax.dynamic_slice_in_dim(queries, start, block, 0)
        scores = block_scores(query_rows, keys_all, start, scale)
        top = jnp.max(scores, axis=-1, keepdims=True)
        expo = jnp.exp(scores - top)
        mass = jnp.sum(expo, axis=-1, keepdims=True)
        weights = (expo / mass).astype(jnp.bfloat16)
        context = jnp.einsum(
            "hbt,the->bhe", weights, values_all, preferred_element_type=jnp.float32
        )
        return (context.astype(jnp.bfloat16), (top + jnp.log(mass))[..., 0])

    contexts, log_mass = lax.map(one_block, jnp.arange(count, dtype=jnp.int32))
    return (contexts.reshape(length, queries.shape[1], queries.shape[2]), log_mass)


def attend_backward(queries, keys_all, values_all, grad_context, log_mass, scale):
    length = queries.shape[0]
    block = min(512, length)
    count = length // block

    def one_block(carry, index):
        grad_keys, grad_values = carry
        start = index * block
        query_rows = lax.dynamic_slice_in_dim(queries, start, block, 0)
        grad_rows = lax.dynamic_slice_in_dim(grad_context, start, block, 0)
        scores = block_scores(query_rows, keys_all, start, scale)
        weights = jnp.exp(scores - log_mass[index][..., None])
        grad_values = grad_values + jnp.einsum(
            "hbt,bhe->the",
            weights.astype(jnp.bfloat16),
            grad_rows,
            preferred_element_type=jnp.float32,
        )
        grad_weights = jnp.einsum(
            "bhe,the->hbt", grad_rows, values_all, preferred_element_type=jnp.float32
        )
        inner = jnp.sum(weights * grad_weights, axis=-1, keepdims=True)
        grad_scores = (weights * (grad_weights - inner)).astype(jnp.bfloat16)
        grad_query = (
            jnp.einsum("hbt,the->bhe", grad_scores, keys_all, preferred_element_type=jnp.float32)
            * scale
        )
        grad_keys = (
            grad_keys
            + jnp.einsum(
                "hbt,bhe->the", grad_scores, query_rows, preferred_element_type=jnp.float32
            )
            * scale
        )
        return ((grad_keys, grad_values), grad_query)

    empty = jnp.zeros(keys_all.shape, jnp.float32)
    (grad_keys, grad_values), grad_queries = lax.scan(
        one_block, (empty, empty), jnp.arange(count, dtype=jnp.int32)
    )
    return (grad_queries.reshape(queries.shape), grad_keys, grad_values)


def per_device(
    tokens,
    w_qkv,
    b_qkv,
    w_out,
    w_up,
    b_up,
    w_down,
    out_bias,
    ln1_gain,
    ln1_shift,
    ln2_gain,
    ln2_shift,
    cotangent,
):
    local_rows = tokens.astype(jnp.float32)
    share = local_rows.shape[0]
    gain_one = ln1_gain.astype(jnp.float32)
    gain_two = ln2_gain.astype(jnp.float32)
    shift_one = ln1_shift.astype(jnp.float32)
    shift_two = ln2_shift.astype(jnp.float32)
    rows_all = gather_rows(tokens).astype(jnp.float32)
    normalized_all, inverse_all = normalize(rows_all)
    first_all = (normalized_all * gain_one + shift_one).astype(jnp.bfloat16)
    second_all = (normalized_all * gain_two + shift_two).astype(jnp.bfloat16)
    offset = lax.axis_index("tensor") * share
    normalized = lax.dynamic_slice_in_dim(normalized_all, offset, share, 0)
    inverse = lax.dynamic_slice_in_dim(inverse_all, offset, share, 0)
    token_count = first_all.shape[0]
    sequences = token_count // LEN
    heads_here = w_qkv.shape[1]
    head_size = w_qkv.shape[2] // 3
    scale = head_size ** (-0.5)
    cosine, sine = rotary_tables(LEN, ROT)
    projected = jnp.einsum(
        "td,dhe->the", first_all, w_qkv, preferred_element_type=jnp.float32
    ) + b_qkv.astype(jnp.float32)
    projected = projected.reshape(sequences, LEN, heads_here, 3 * head_size)
    queries = rotate(projected[..., :head_size], cosine, sine, ROT).astype(jnp.bfloat16)
    keys_bf = rotate(projected[..., head_size : 2 * head_size], cosine, sine, ROT).astype(
        jnp.bfloat16
    )
    values_bf = projected[..., 2 * head_size :].astype(jnp.bfloat16)

    def forward_sequence(group):
        return attend_forward(group[0], group[1], group[2], scale)

    contexts, log_mass = lax.map(forward_sequence, (queries, keys_bf, values_bf))
    context_flat = contexts.reshape(token_count, heads_here * head_size)
    hidden = jnp.dot(second_all, w_up, preferred_element_type=jnp.float32) + b_up.astype(
        jnp.float32
    )
    activated = jax.nn.gelu(hidden, approximate=False).astype(jnp.bfloat16)
    out_flat = w_out.reshape(heads_here * head_size, w_out.shape[2])
    branch_total = scatter_rows(
        (
            jnp.dot(context_flat, out_flat, preferred_element_type=jnp.float32)
            + jnp.dot(activated, w_down, preferred_element_type=jnp.float32)
        ).astype(jnp.bfloat16)
    )
    layer_out = (local_rows + branch_total + out_bias.astype(jnp.float32)).astype(jnp.bfloat16)
    grad_all = gather_rows(cotangent)
    grad_active = jnp.einsum("td,fd->tf", grad_all, w_down, preferred_element_type=jnp.float32)
    grad_w_down = jnp.einsum("tf,td->fd", activated, grad_all, preferred_element_type=jnp.float32)
    gelu_value, gelu_pull = jax.vjp(partial(jax.nn.gelu, approximate=False), hidden)
    grad_hidden = gelu_pull(grad_active)[0].astype(jnp.bfloat16)
    grad_b_up = jnp.sum(grad_hidden.astype(jnp.float32), axis=0)
    grad_w_up = jnp.einsum("td,tf->df", second_all, grad_hidden, preferred_element_type=jnp.float32)
    grad_second = jnp.einsum("tf,df->td", grad_hidden, w_up, preferred_element_type=jnp.float32)
    context_heads = contexts.reshape(token_count, heads_here, head_size)
    grad_context = jnp.einsum(
        "td,hed->the", grad_all, w_out, preferred_element_type=jnp.float32
    ).astype(jnp.bfloat16)
    grad_w_out = jnp.einsum(
        "the,td->hed", context_heads, grad_all, preferred_element_type=jnp.float32
    )
    grad_context = grad_context.reshape(sequences, LEN, heads_here, head_size)

    def backward_sequence(group):
        return attend_backward(group[0], group[1], group[2], group[3], group[4], scale)

    grad_queries, grad_keys, grad_values = lax.map(
        backward_sequence, (queries, keys_bf, values_bf, grad_context, log_mass)
    )
    grad_projected = jnp.concatenate(
        [
            rotate(grad_queries, cosine, -sine, ROT),
            rotate(grad_keys, cosine, -sine, ROT),
            grad_values,
        ],
        axis=-1,
    )
    grad_projected = grad_projected.astype(jnp.bfloat16).reshape(
        token_count, heads_here, 3 * head_size
    )
    grad_b_qkv = jnp.sum(grad_projected.astype(jnp.float32), axis=0)
    grad_w_qkv = jnp.einsum(
        "td,the->dhe", first_all, grad_projected, preferred_element_type=jnp.float32
    )
    grad_first = jnp.einsum(
        "the,dhe->td", grad_projected, w_qkv, preferred_element_type=jnp.float32
    )
    grad_rows = cotangent.astype(jnp.float32)
    partial_sums = (
        jnp.sum(grad_rows, axis=0),
        jnp.sum(grad_first * normalized_all, axis=0),
        jnp.sum(grad_first, axis=0),
        jnp.sum(grad_second * normalized_all, axis=0),
        jnp.sum(grad_second, axis=0),
    )
    weighted = grad_first * gain_one + grad_second * gain_two
    local_weighted = scatter_rows(weighted.astype(jnp.bfloat16))
    input_grad = (grad_rows + norm_back(local_weighted, normalized, inverse)).astype(jnp.bfloat16)
    small_sums = sum_all(jnp.stack(partial_sums))
    low = jnp.bfloat16
    ff_here = w_up.shape[1]
    model = w_up.shape[0]
    quarter = model // 4
    head_rows = heads_here * head_size
    widths = heads_here * 3 * head_size

    def by_columns(grad):
        return jnp.swapaxes(grad.reshape(grad.shape[0], 4, quarter), 0, 1)

    def from_columns(chunks):
        return jnp.swapaxes(chunks, 0, 1).reshape(chunks.shape[1], model)

    feed = jnp.concatenate(
        [
            grad_w_up.reshape(4, quarter, ff_here),
            by_columns(grad_w_down),
            jnp.broadcast_to(grad_b_up[None, None, :], (4, 16, ff_here)),
        ],
        axis=1,
    ).astype(low)
    feed = sum_dp(feed)
    head_parts = jnp.concatenate(
        [
            jnp.pad(
                grad_w_qkv.reshape(4, quarter, widths), ((0, 0), (0, 0), (0, quarter - widths))
            ),
            by_columns(grad_w_out.reshape(head_rows, model)),
            jnp.broadcast_to(
                jnp.pad(grad_b_qkv.reshape(widths), (0, quarter - widths))[None, None, :],
                (4, 16, quarter),
            ),
        ],
        axis=1,
    ).astype(low)
    head_parts = sum_dp(head_parts)
    large_sums = (
        head_parts[:, :quarter, :widths].reshape(grad_w_qkv.shape),
        head_parts[0, quarter + head_rows, :widths].reshape(grad_b_qkv.shape),
        from_columns(head_parts[:, quarter : quarter + head_rows]).reshape(grad_w_out.shape),
        feed[:, :quarter].reshape(grad_w_up.shape),
        feed[0, 2 * quarter],
        from_columns(feed[:, quarter : 2 * quarter]),
    )
    return (
        layer_out,
        input_grad,
        large_sums[0],
        large_sums[1],
        large_sums[2],
        large_sums[3],
        large_sums[4],
        large_sums[5],
        small_sums[0],
        small_sums[1],
        small_sums[2],
        small_sums[3],
        small_sums[4],
    )


def solution(mesh):
    placed = (
        P(("dp", "tensor"), None),
        P(None, "tensor", None),
        P("tensor", None),
        P("tensor", None, None),
        P(None, "tensor"),
        P("tensor"),
        P("tensor", None),
        P(),
        P(),
        P(),
        P(),
        P(),
        P(("dp", "tensor"), None),
    )
    return jax.shard_map(
        per_device,
        mesh=mesh,
        in_specs=placed,
        out_specs=(
            P(("dp", "tensor"), None),
            P(("dp", "tensor"), None),
            P(None, "tensor", None),
            P("tensor", None),
            P("tensor", None, None),
            P(None, "tensor"),
            P("tensor"),
            P("tensor", None),
            P(),
            P(),
            P(),
            P(),
            P(),
        ),
        check_vma=False,
    )
```

```python
from functools import partial

import jax
import jax.numpy as jnp
import numpy as np
from jax import lax
from jax.experimental import pallas as pl
from jax.experimental.pallas import tpu as pltpu
from jax.sharding import PartitionSpec as P

ROT = 16
LEN = 2048
EPS = 1e-05
HEAD = 64
ROWS = 256
STEPS = LEN // ROWS
HALF = ROWS // 2
SCALE = HEAD ** (-0.5)
EXTRA = 16

SAME_CORE = [[c + 2 * i for i in range(8)] for c in range(2)]
PAIR = [(i, i ^ 1) for i in range(16)]
Z_PAIR = [(i, i ^ 1) for i in range(8)]

F32 = jnp.float32
LOW = jnp.bfloat16


def swap_core(value):
    return lax.ppermute(value, "tensor", PAIR)


def trade_chips(blocks):
    return lax.all_to_all(blocks, "tensor", 0, 0, axis_index_groups=SAME_CORE, tiled=True)


def copies(block, count):
    return jnp.broadcast_to(block[None], (count,) + block.shape)


def move_x(value, distance):
    pairs = [(i, (i // 2 + distance) % 4 * 2 + i % 2) for i in range(8)]
    return lax.ppermute(value, "dp", pairs)


def add_four(own, moved):
    total = own.astype(F32)
    for part in moved:
        total = total + part.astype(F32)
    return total.astype(LOW)


def sum_z(low):
    other = lax.ppermute(low, "dp", Z_PAIR)
    return (low.astype(F32) + other.astype(F32)).astype(LOW)


def spread_x(low):
    return [low] + [move_x(low, distance) for distance in range(1, 4)]


def sum_four(rows, move):
    return (rows + move(rows, 2)) + (move(rows, 1) + move(rows, 3))


def normalize(values):
    center = values - jnp.mean(values, axis=-1, keepdims=True)
    inverse = lax.rsqrt(jnp.mean(center * center, axis=-1, keepdims=True) + EPS)
    return (center * inverse, inverse)


def norm_back(scaled, normalized, inverse):
    centered = scaled - jnp.mean(scaled, axis=-1, keepdims=True)
    return inverse * (centered - normalized * jnp.mean(scaled * normalized, axis=-1, keepdims=True))


def rotary_tables():
    lane = np.arange(2 * HEAD) % HEAD
    half = ROT // 2
    inverse = np.float32(10000.0) ** (-2.0 * (lane % half).astype(np.float32) / np.float32(ROT))
    inverse = np.where(lane < ROT, inverse, 0.0).astype(np.float32)
    angles = np.arange(LEN, dtype=np.float32)[:, None] * inverse[None, :]
    sign = np.where(lane < half, -1.0, 1.0).astype(np.float32)
    return np.cos(angles).astype(np.float32), (np.sin(angles) * sign).astype(np.float32)


def turn(values, cosine, sine):
    lane = lax.broadcasted_iota(jnp.int32, values.shape, 1) % HEAD
    partner = jnp.where(
        lane < ROT // 2,
        pltpu.roll(values, 2 * HEAD - ROT // 2, 1),
        pltpu.roll(values, ROT // 2, 1),
    )
    return values * cosine + partner * sine


def dot(left, right, left_axis=1, right_axis=0):
    return lax.dot_general(
        left,
        right,
        (((left_axis,), (right_axis,)), ((), ())),
        preferred_element_type=F32,
    )


def core_here():
    return lax.axis_index("tensor") % 2


def join_rows(mine, other, rows):
    core = core_here()
    rows[pl.ds(pl.multiple_of(core * HALF, HALF), HALF), :] = mine[0]
    rows[pl.ds(pl.multiple_of((1 - core) * HALF, HALF), HALF), :] = other[0]


def send_rows(block, send):
    core = core_here()
    send[0] = block[pl.ds(pl.multiple_of((1 - core) * HALF, HALF), HALF), :]


def x_here():
    return lax.axis_index("dp") // 2


def row_sum(values):
    return jnp.sum(values, axis=0, keepdims=True)


def project_kernel(
    mine, other, vecs, w_qkv, b_qkv, w_up, b_up, cosine, sine,
    first, second, normal, queries, keys, values, active, active_send, slope, rows,
):
    join_rows(mine, other, rows)
    here = rows[...].astype(F32)
    mean = jnp.mean(here, axis=-1, keepdims=True)
    center = here - mean
    inverse = lax.rsqrt(jnp.mean(center * center, axis=-1, keepdims=True) + EPS)
    normalized = center * inverse
    normal[...] = normalized.astype(LOW)
    one = (normalized * vecs[0:1, :] + vecs[1:2, :]).astype(LOW)
    two = (normalized * vecs[2:3, :] + vecs[3:4, :]).astype(LOW)
    first[...] = one
    second[...] = two
    projected = dot(one, w_qkv[...], 1, 1) + b_qkv[...]
    turned = turn(projected[:, : 2 * HEAD], cosine[...], sine[...])
    queries[...] = turned[:, :HEAD].astype(LOW) * SCALE
    keys[...] = turned[:, HEAD:].astype(LOW)
    values[...] = projected[:, 2 * HEAD :].astype(LOW)
    hidden = dot(two, w_up[...]) + b_up[...]
    share = 0.5 * (1.0 + lax.erf(hidden * (0.5**0.5)))
    active[...] = (hidden * share).astype(LOW)
    send_rows(active, active_send)
    slope[...] = share + hidden * (jnp.exp(-0.5 * hidden * hidden) * ((2.0 * np.pi) ** -0.5))


def attend_kernel(queries, keys, values, context, context_send, mass):
    place = lax.broadcasted_iota(jnp.int32, (ROWS, ROWS), 0)
    query = lax.broadcasted_iota(jnp.int32, (ROWS, ROWS), 1)
    seen = place <= query

    def block(index):
        low, high = index * ROWS, (index + 1) * ROWS
        asked = queries[low:high, :]
        near = jnp.where(seen, dot(keys[low:high, :], asked, 1, 1), -1e30)
        top = jnp.max(near, axis=0, keepdims=True)
        if index:
            far = dot(keys[:low, :], asked, 1, 1)
            top = jnp.maximum(top, jnp.max(far, axis=0, keepdims=True))
            far = jnp.exp(far - top)
        near = jnp.exp(near - top)
        total = row_sum(near)
        if index:
            total = total + row_sum(far)
        scale = 1.0 / total
        mass[0] = top + jnp.log(total)
        found = dot(values[low:high, :], (near * scale).astype(LOW), 0, 0)
        if index:
            found = found + dot(values[:low, :], (far * scale).astype(LOW), 0, 0)
        context[...] = found.T.astype(LOW)

    for index in range(STEPS):
        pl.when(pl.program_id(0) == index)(partial(block, index))
    send_rows(context, context_send)


def flat(block):
    return block.reshape(ROWS, block.shape[-1])


def mix_kernel(
    core, context, active, context_in, active_in, w_out, w_down, w_out_in, w_down_in, result
):
    mixed = dot(flat(context[...]), w_out[...]) + dot(flat(active[...]), w_down[...])
    mixed = mixed + dot(flat(context_in[...]), w_out_in[...])
    mixed = mixed + dot(flat(active_in[...]), w_down_in[...])
    result[...] = mixed.astype(LOW).reshape(2, HALF, mixed.shape[1])


def feed_back_kernel(
    mine, other, active, slope, second, context, w_down, w_out,
    grad_hidden, hidden_send, grad_context, feed_0, feed_1, feed_2, feed_3, grad_out,
    rows, up_sum, down_sum, out_sum, bias_sum,
):
    step = pl.program_id(0)

    @pl.when(step == 0)
    def _():
        up_sum[...] = jnp.zeros_like(up_sum)
        down_sum[...] = jnp.zeros_like(down_sum)
        out_sum[...] = jnp.zeros_like(out_sum)
        bias_sum[...] = jnp.zeros_like(bias_sum)

    join_rows(mine, other, rows)
    grads = rows[...]
    hidden = (dot(grads, w_down[...], 1, 1) * slope[...]).astype(LOW)
    grad_hidden[...] = hidden
    send_rows(grad_hidden, hidden_send)
    grad_context[...] = dot(grads, w_out[...], 1, 1).astype(LOW)
    down_sum[...] += dot(active[...], grads, 0, 0)
    out_sum[...] += dot(context[...], grads, 0, 0)
    up_sum[...] += dot(hidden, second[...], 0, 0)
    bias_sum[...] += row_sum(hidden.astype(F32))

    @pl.when(step == STEPS - 1)
    def _():
        grad_out[...] = out_sum[...].astype(LOW)
        for slot, feed in enumerate((feed_0, feed_1, feed_2, feed_3)):
            span = quarter((x_here() + slot) % 4)
            feed[0:256, :] = up_sum[:, span].T.astype(LOW)
            feed[256:512, :] = down_sum[:, span].astype(LOW)
            feed[512:528, :] = jnp.broadcast_to(bias_sum[...], (16, 256)).astype(LOW)


def quarter(part):
    return pl.ds(pl.multiple_of(part * 256, 256), 256)


def attend_back_kernel(
    queries, keys, values, grad_context, mass, cosine, sine,
    grad_projected, projected_send, query_sum, key_sum, value_sum,
):
    place = lax.broadcasted_iota(jnp.int32, (ROWS, ROWS), 0)
    query = lax.broadcasted_iota(jnp.int32, (ROWS, ROWS), 1)
    seen = place <= query

    @pl.when(pl.program_id(0) == 0)
    def _():
        key_sum[...] = jnp.zeros_like(key_sum)
        value_sum[...] = jnp.zeros_like(value_sum)

    def block(index):
        low, high = index * ROWS, (index + 1) * ROWS
        asked = queries[low:high, :]
        grads = grad_context[...]
        spans = [slice(low, high)] + ([slice(0, low)] if index else [])
        weights, pulls = [], []
        inner = 0.0
        for number, span in enumerate(spans):
            scores = dot(keys[span, :], asked, 1, 1)
            if number == 0:
                scores = jnp.where(seen, scores, -1e30)
            weight = jnp.exp(scores - mass[0])
            pull = dot(values[span, :], grads, 1, 1)
            inner = inner + row_sum(weight * pull)
            weights.append(weight)
            pulls.append(pull)
        asked_grad = 0.0
        for span, weight, pull in zip(spans, weights, pulls):
            value_sum[span, :] += dot(weight.astype(LOW), grads)
            scores_grad = (weight * (pull - inner)).astype(LOW)
            key_sum[span, :] += dot(scores_grad, asked)
            asked_grad = asked_grad + dot(keys[span, :], scores_grad, 0, 0)
        query_sum[low:high, :] = asked_grad.T * SCALE

    for index in range(STEPS):
        pl.when(pl.program_id(0) == index)(partial(block, index))

    @pl.when(pl.program_id(0) == STEPS - 1)
    def _():
        for index in range(STEPS):
            span = slice(index * ROWS, (index + 1) * ROWS)
            both = jnp.concatenate([query_sum[span, :], key_sum[span, :]], axis=1)
            turned = turn(both, cosine[span, :], -sine[span, :])
            grad_projected[span, : 2 * HEAD] = turned.astype(LOW)
            grad_projected[span, 2 * HEAD :] = value_sum[span, :].astype(LOW)
            place = index * ROWS + (1 - core_here()) * HALF
            projected_send[index] = grad_projected[pl.ds(pl.multiple_of(place, HALF), HALF), :]


def input_back_kernel(
    core, projected, hidden, projected_in, hidden_in, vecs, w_qkv, w_up, w_qkv_in, w_up_in, sums,
    result,
):
    one = dot(flat(projected[...]), w_qkv[...])
    one = one + dot(flat(projected_in[...]), w_qkv_in[...])
    two = dot(flat(hidden[...]), w_up[...], 1, 1)
    two = two + dot(flat(hidden_in[...]), w_up_in[...], 1, 1)
    weighted = one * vecs[0:1, :] + two * vecs[2:3, :]
    result[:, 0:HALF, :] = weighted.astype(LOW).reshape(2, HALF, weighted.shape[1])
    high = sums[...].astype(LOW).astype(F32)
    rest = jnp.zeros((EXTRA - 10, weighted.shape[1]), F32)
    tail = jnp.concatenate([high, sums[...] - high, rest], axis=0).astype(LOW)
    result[0, HALF:, :] = tail
    result[1, HALF:, :] = tail


def dot_full(left, right, right_axis):
    return lax.dot_general(
        left,
        right.astype(F32),
        (((1,), (right_axis,)), ((), ())),
        precision=lax.Precision.HIGHEST,
        preferred_element_type=F32,
    )


def last_grads_kernel(
    grad_projected, grad_hidden, first, normal, grad_out, w_qkv, w_up, own_sum,
    head_0, head_1, head_2, head_3, sums, qkv_sum, moments, bias_sum,
):
    step = pl.program_id(0)
    wide = 3 * HEAD

    @pl.when(step == 0)
    def _():
        qkv_sum[...] = jnp.zeros_like(qkv_sum)
        moments[...] = jnp.zeros_like(moments)
        bias_sum[...] = jnp.zeros_like(bias_sum)

    grads = grad_projected[...]
    hidden = grad_hidden[...]
    qkv_sum[...] += dot(grads, first[...], 0, 0)
    moments[0:wide, :] += dot(grads, normal[...], 0, 0)
    moments[wide:, :] += dot(hidden, normal[...], 0, 0)
    bias_sum[:, 0:wide] += row_sum(grads.astype(F32))
    bias_sum[:, 256:] += row_sum(hidden.astype(F32))

    @pl.when(step == STEPS - 1)
    def _():
        bias = bias_sum[:, 0:wide]
        for slot, head in enumerate((head_0, head_1, head_2, head_3)):
            span = quarter((x_here() + slot) % 4)
            head[0:wide, :] = qkv_sum[:, span].astype(LOW)
            head[wide:256, :] = grad_out[:, span]
            head[256:272, :wide] = jnp.broadcast_to(bias, (16, wide)).astype(LOW)
            head[256:272, wide:] = jnp.zeros((16, 256 - wide), LOW)
        sums[0:1, :] = row_sum(moments[0:wide, :] * w_qkv[...].astype(F32))
        sums[1:2, :] = dot_full(bias, w_qkv[...], 0)
        sums[2:3, :] = row_sum(moments[wide:, :] * w_up[...].astype(F32).T)
        sums[3:4, :] = dot_full(bias_sum[:, 256:], w_up[...], 1)
        sums[4:5, :] = own_sum[...]


def finish_grads_kernel(
    feed_0, feed_1, feed_2, feed_3, head_0, head_1, head_2, head_3,
    grad_qkv, grad_qkv_bias, grad_out, grad_up, grad_up_bias, grad_down,
):
    wide = 3 * HEAD
    for slot, feed in enumerate((feed_0, feed_1, feed_2, feed_3)):
        span = quarter((x_here() + 4 - slot) % 4)
        grad_up[span, :] = feed[0:256, :].astype(F32)
        grad_down[:, span] = feed[256:512, :].astype(F32)
    for slot, head in enumerate((head_0, head_1, head_2, head_3)):
        span = quarter((x_here() + 4 - slot) % 4)
        grad_qkv[:, span] = head[0:wide, :].astype(F32)
        grad_out[:, span] = head[wide:256, :].astype(F32)
    grad_up_bias[...] = feed_0[512:513, :].astype(F32)
    grad_qkv_bias[...] = head_0[256:257, :wide].astype(F32)


def finish_out_kernel(parts, tokens, out_bias, layer_out):
    total = jnp.sum(parts[...].astype(F32), axis=0)
    layer_out[...] = (tokens[...].astype(F32) + total + out_bias[...].astype(F32)).astype(LOW)


def finish_back_kernel(parts, tokens, cotangent, input_grad, sums):
    scaled = jnp.sum(parts[:, 0:HALF, :].astype(F32), axis=0)
    normalized, inverse = normalize(tokens[...].astype(F32))
    input_grad[...] = (
        cotangent[...].astype(F32) + norm_back(scaled, normalized, inverse)
    ).astype(LOW)
    tail = jnp.sum(parts[:, HALF:, :].astype(F32), axis=0)
    sums[...] = tail[0:5] + tail[5:10]


def whole(shape):
    return pl.BlockSpec(shape, lambda step: (0,) * len(shape))


def by_rows(columns):
    return pl.BlockSpec((ROWS, columns), lambda step: (step, 0))


HALVES = pl.BlockSpec((1, HALF, 1024), lambda step: (step, 0, 0))
MASS = pl.BlockSpec((1, 1, ROWS), lambda step: (step, 0, 0))


def shape(dims, kind):
    return jax.ShapeDtypeStruct(dims, kind)


COST = pl.CostEstimate(flops=1, bytes_accessed=1, transcendentals=0)


def launch(kernel, name, ins, outs, out_shapes, scratch, steps=STEPS, scalars=0):
    return pl.pallas_call(
        kernel,
        name=name,
        grid_spec=pltpu.PrefetchScalarGridSpec(
            num_scalar_prefetch=scalars,
            grid=(steps,),
            in_specs=ins,
            out_specs=outs,
            scratch_shapes=scratch,
        ),
        out_shape=out_shapes,
        compiler_params=pltpu.CompilerParams(vmem_limit_bytes=40 * 2**20),
        cost_estimate=COST,
    )


def fixed(dims):
    return pl.BlockSpec(dims, lambda step, core: (0,) * len(dims))


def parity(columns):
    return pl.BlockSpec((2, 1, HALF, columns), lambda step, core: (step, core[0], 0, 0))


def double(columns):
    return pl.BlockSpec((2, HALF, columns), lambda step, core: (step, 0, 0))


def half_rows(columns):
    return pl.BlockSpec((1, HALF, columns), lambda step: (step, 0, 0))


def four(value):
    return value.reshape(STEPS, 2, HALF, value.shape[1])


def per_device(
    tokens, w_qkv, b_qkv, w_out, w_up, b_up, w_down, out_bias,
    ln1_gain, ln1_shift, ln2_gain, ln2_shift, cotangent,
):
    model = w_up.shape[0]
    feed_here = w_up.shape[1]
    wide = 3 * HEAD
    core = core_here().astype(jnp.int32).reshape(1)
    w_qkv = w_qkv.transpose(1, 2, 0).reshape(wide, model)
    w_out = w_out.reshape(HEAD, model)
    vecs = jnp.stack([ln1_gain, ln1_shift, ln2_gain, ln2_shift]).astype(F32)
    cosine, sine = rotary_tables()
    own_sum = jnp.sum(cotangent.astype(F32), axis=0)[None, :]

    held = copies(cotangent, 8)
    mine = trade_chips(copies(tokens, 8))
    weights_in = [swap_core(w) for w in (w_out, w_down, w_qkv, w_up)]
    held, vecs, b_qkv, b_up, core, own_sum, mine, *weights_in = lax.optimization_barrier(
        (held, vecs, b_qkv.astype(F32), b_up.astype(F32)[None, :], core, own_sum, mine)
        + tuple(weights_in)
    )
    w_out_in, w_down_in, w_qkv_in, w_up_in = weights_in
    other = swap_core(mine)
    grad_mine = trade_chips(held)

    halves = shape((STEPS, HALF, feed_here), LOW)
    first, second, normal, queries, keys, values, active, active_send, slope = launch(
        project_kernel,
        "project",
        [
            HALVES, HALVES, whole((4, model)), whole((wide, model)), whole((1, wide)),
            whole((model, feed_here)), whole((1, feed_here)), by_rows(128), by_rows(128),
        ],
        [
            by_rows(model), by_rows(model), by_rows(model), by_rows(HEAD), by_rows(HEAD),
            by_rows(HEAD), by_rows(feed_here), half_rows(feed_here), by_rows(feed_here),
        ],
        [
            shape((LEN, model), LOW), shape((LEN, model), LOW), shape((LEN, model), LOW),
            shape((LEN, HEAD), LOW), shape((LEN, HEAD), LOW), shape((LEN, HEAD), LOW),
            shape((LEN, feed_here), LOW), halves, shape((LEN, feed_here), F32),
        ],
        [pltpu.VMEM((ROWS, model), LOW)],
    )(mine, other, vecs, w_qkv, b_qkv, w_up, b_up, cosine, sine)
    active_in = swap_core(active_send)

    context, context_send, mass = launch(
        attend_kernel,
        "attend",
        [whole((LEN, HEAD))] * 3,
        [by_rows(HEAD), half_rows(HEAD), MASS],
        [
            shape((LEN, HEAD), LOW), shape((STEPS, HALF, HEAD), LOW),
            shape((STEPS, 1, ROWS), F32),
        ],
        [],
    )(queries, keys, values)
    context_in = swap_core(context_send)

    mixed = launch(
        mix_kernel,
        "mix",
        [
            parity(HEAD), parity(feed_here), double(HEAD), double(feed_here),
            fixed((HEAD, model)), fixed((feed_here, model)),
            fixed((HEAD, model)), fixed((feed_here, model)),
        ],
        double(model),
        shape((STEPS, HALF, model), LOW),
        [],
        steps=4,
        scalars=1,
    )(
        core, four(context), four(active), context_in, active_in,
        w_out, w_down, w_out_in, w_down_in,
    )

    grad_mine, mixed = lax.optimization_barrier((grad_mine, mixed))
    grad_other = swap_core(grad_mine)
    branch = trade_chips(mixed)

    grad_hidden, hidden_send, grad_context, *feed, grad_out = launch(
        feed_back_kernel,
        "feed_back",
        [
            HALVES, HALVES, by_rows(feed_here), by_rows(feed_here), by_rows(model),
            by_rows(HEAD), whole((feed_here, model)), whole((HEAD, model)),
        ],
        [by_rows(feed_here), half_rows(feed_here), by_rows(HEAD)]
        + [whole((528, 256))] * 4 + [whole((HEAD, model))],
        [shape((LEN, feed_here), LOW), halves, shape((LEN, HEAD), LOW)]
        + [shape((528, 256), LOW)] * 4 + [shape((HEAD, model), LOW)],
        [
            pltpu.VMEM((ROWS, model), LOW), pltpu.VMEM((feed_here, model), F32),
            pltpu.VMEM((feed_here, model), F32), pltpu.VMEM((HEAD, model), F32),
            pltpu.VMEM((1, feed_here), F32),
        ],
    )(grad_mine, grad_other, active, slope, second, context, w_down, w_out)
    hidden_in = swap_core(hidden_send)
    feed_moved = [move_x(feed[distance], distance) for distance in range(1, 4)]

    grad_projected, projected_send = launch(
        attend_back_kernel,
        "attend_back",
        [
            whole((LEN, HEAD)), whole((LEN, HEAD)), whole((LEN, HEAD)), by_rows(HEAD), MASS,
            whole((LEN, 128)), whole((LEN, 128)),
        ],
        [whole((LEN, wide)), whole((STEPS, HALF, wide))],
        [shape((LEN, wide), LOW), shape((STEPS, HALF, wide), LOW)],
        [pltpu.VMEM((LEN, HEAD), F32)] * 3,
    )(queries, keys, values, grad_context, mass, cosine, sine)
    grad_projected, projected_send, branch, hidden_in, *feed_moved = lax.optimization_barrier(
        (grad_projected, projected_send, branch, hidden_in, *feed_moved)
    )
    projected_in = swap_core(projected_send)
    feed_low = sum_z(add_four(feed[0], feed_moved))

    *head, sums = launch(
        last_grads_kernel,
        "last_grads",
        [
            by_rows(wide), by_rows(feed_here), by_rows(model), by_rows(model),
            whole((HEAD, model)), whole((wide, model)), whole((model, feed_here)),
            whole((1, model)),
        ],
        [whole((272, 256))] * 4 + [whole((5, model))],
        [shape((272, 256), LOW)] * 4 + [shape((5, model), F32)],
        [
            pltpu.VMEM((wide, model), F32), pltpu.VMEM((wide + feed_here, model), F32),
            pltpu.VMEM((1, 512), F32),
        ],
    )(grad_projected, grad_hidden, first, normal, grad_out, w_qkv, w_up, own_sum)
    sums = sums + swap_core(sums)
    head_moved = [move_x(head[distance], distance) for distance in range(1, 4)]

    both = launch(
        input_back_kernel,
        "input_back",
        [
            parity(wide), parity(feed_here), double(wide), double(feed_here), fixed((4, model)),
            fixed((wide, model)), fixed((model, feed_here)),
            fixed((wide, model)), fixed((model, feed_here)), fixed((5, model)),
        ],
        pl.BlockSpec((2, HALF + EXTRA, model), lambda step, core: (step, 0, 0)),
        shape((STEPS, HALF + EXTRA, model), LOW),
        [],
        steps=4,
        scalars=1,
    )(
        core, four(grad_projected), four(grad_hidden), projected_in, hidden_in, vecs,
        w_qkv, w_up, w_qkv_in, w_up_in, sums,
    )
    both, feed_low, *head_moved = lax.optimization_barrier((both, feed_low, *head_moved))
    scaled = trade_chips(both)
    head_low = sum_z(add_four(head[0], head_moved))
    feed_parts = spread_x(feed_low)
    head_parts = spread_x(head_low)

    layer_out = pl.pallas_call(
        finish_out_kernel,
        name="finish_out",
        out_shape=shape(tokens.shape, LOW),
        cost_estimate=COST,
    )(branch, tokens, out_bias[None, :])
    grad_qkv, grad_qkv_bias, grad_out, grad_up, grad_up_bias, grad_down = pl.pallas_call(
        finish_grads_kernel,
        name="finish_grads",
        out_shape=[
            shape((wide, model), F32), shape((1, wide), F32), shape((HEAD, model), F32),
            shape((model, feed_here), F32), shape((1, feed_here), F32),
            shape((feed_here, model), F32),
        ],
        cost_estimate=COST,
    )(*feed_parts, *head_parts)
    input_grad, small = pl.pallas_call(
        finish_back_kernel,
        name="finish_back",
        out_shape=[shape(tokens.shape, LOW), shape((5, model), F32)],
        cost_estimate=COST,
    )(scaled, tokens, cotangent)
    small = sum_four(small + lax.ppermute(small, "dp", Z_PAIR), move_x)

    return (
        layer_out,
        input_grad,
        grad_qkv.reshape(1, wide, model).transpose(2, 0, 1),
        grad_qkv_bias,
        grad_out.reshape(1, HEAD, model),
        grad_up,
        grad_up_bias[0],
        grad_down,
        small[4],
        small[0],
        small[1],
        small[2],
        small[3],
    )


def solution(mesh):
    placed = (
        P(("dp", "tensor"), None),
        P(None, "tensor", None),
        P("tensor", None),
        P("tensor", None, None),
        P(None, "tensor"),
        P("tensor"),
        P("tensor", None),
        P(),
        P(),
        P(),
        P(),
        P(),
        P(("dp", "tensor"), None),
    )
    return jax.shard_map(
        per_device,
        mesh=mesh,
        in_specs=placed,
        out_specs=(
            P(("dp", "tensor"), None),
            P(("dp", "tensor"), None),
            P(None, "tensor", None),
            P("tensor", None),
            P("tensor", None, None),
            P(None, "tensor"),
            P("tensor"),
            P("tensor", None),
            P(),
            P(),
            P(),
            P(),
            P(),
        ),
        check_vma=False,
    )
```

```python
from functools import partial

import jax
import jax.numpy as jnp
import numpy as np
from jax import lax
from jax.experimental import pallas as pl
from jax.experimental.pallas import tpu as pltpu
from jax.sharding import PartitionSpec as P

ROT = 16
LEN = 2048
EPS = 1e-05
HEAD = 64
ROWS = 256
STEPS = LEN // ROWS
HALF = ROWS // 2
SCALE = HEAD ** (-0.5)
EXTRA = 16

SAME_CORE = [[c + 2 * i for i in range(8)] for c in range(2)]
PAIR = [(i, i ^ 1) for i in range(16)]
Z_PAIR = [(i, i ^ 1) for i in range(8)]

F32 = jnp.float32
LOW = jnp.bfloat16


def swap_core(value):
    return lax.ppermute(value, "tensor", PAIR)


def trade_chips(blocks):
    return lax.all_to_all(blocks, "tensor", 0, 0, axis_index_groups=SAME_CORE, tiled=True)


def copies(block, count):
    return jnp.broadcast_to(block[None], (count,) + block.shape)


def move_x(value, distance):
    pairs = [(i, (i // 2 + distance) % 4 * 2 + i % 2) for i in range(8)]
    return lax.ppermute(value, "dp", pairs)


def add_four(own, moved):
    total = own.astype(F32)
    for part in moved:
        total = total + part.astype(F32)
    return total.astype(LOW)


def add_low(left, right):
    return (left.astype(F32) + right.astype(F32)).astype(LOW)


def sum_z(low):
    return add_low(low, lax.ppermute(low, "dp", Z_PAIR))


def spread_x(low):
    return [low] + [move_x(low, distance) for distance in range(1, 4)]


def sum_four(rows, move):
    return (rows + move(rows, 2)) + (move(rows, 1) + move(rows, 3))


def normalize(values):
    center = values - jnp.mean(values, axis=-1, keepdims=True)
    inverse = lax.rsqrt(jnp.mean(center * center, axis=-1, keepdims=True) + EPS)
    return (center * inverse, inverse)


def norm_back(scaled, normalized, inverse):
    centered = scaled - jnp.mean(scaled, axis=-1, keepdims=True)
    return inverse * (centered - normalized * jnp.mean(scaled * normalized, axis=-1, keepdims=True))


def rotary_tables():
    lane = np.arange(2 * HEAD) % HEAD
    half = ROT // 2
    inverse = np.float32(10000.0) ** (-2.0 * (lane % half).astype(np.float32) / np.float32(ROT))
    inverse = np.where(lane < ROT, inverse, 0.0).astype(np.float32)
    angles = np.arange(LEN, dtype=np.float32)[:, None] * inverse[None, :]
    sign = np.where(lane < half, -1.0, 1.0).astype(np.float32)
    return np.cos(angles).astype(np.float32), (np.sin(angles) * sign).astype(np.float32)


def turn(values, cosine, sine):
    lane = lax.broadcasted_iota(jnp.int32, values.shape, 1) % HEAD
    partner = jnp.where(
        lane < ROT // 2,
        pltpu.roll(values, 2 * HEAD - ROT // 2, 1),
        pltpu.roll(values, ROT // 2, 1),
    )
    return values * cosine + partner * sine


def dot(left, right, left_axis=1, right_axis=0):
    return lax.dot_general(
        left,
        right,
        (((left_axis,), (right_axis,)), ((), ())),
        preferred_element_type=F32,
    )


def core_here():
    return lax.axis_index("tensor") % 2


def stream(count, moves):
    step = pl.program_id(0)

    @pl.when(step == 0)
    def _():
        for place in range(count):
            for move in moves:
                move(place).start()

    for move in moves:
        move(step).wait()


def fetch(source, target, done):
    def move(place):
        return pltpu.make_async_copy(source(place), target(place), done.at[place])

    return move


def fetch_rows(source, target, done):
    return fetch(
        lambda place: source.at[pl.ds(place * ROWS, ROWS)], lambda place: target.at[place], done
    )


def fetch_parity(source, target, done):
    core = core_here()
    return fetch(
        lambda place: source.at[pl.ds(place * 2, 2), core], lambda place: target.at[place], done
    )


def fetch_double(source, target, done):
    return fetch(
        lambda place: source.at[pl.ds(place * 2, 2)], lambda place: target.at[place], done
    )


def fetch_joined(source, target, done, core):
    start = pl.multiple_of(core * HALF, HALF)
    return fetch(
        lambda place: source.at[place],
        lambda place: target.at[place, pl.ds(start, HALF)],
        done,
    )


def send_rows(block, send):
    core = core_here()
    send[0] = block[pl.ds(pl.multiple_of((1 - core) * HALF, HALF), HALF), :]


def x_here():
    return lax.axis_index("dp") // 2


def row_sum(values):
    return jnp.sum(values, axis=0, keepdims=True)


def forward_kernel(
    mine, other, vecs, w_qkv, b_qkv, w_up, b_up, cosine, sine,
    first, second, normal, queries, keys, values, active, active_send, slope,
    context, context_send, mass, rows, mine_done, other_done,
):
    core = core_here()
    stream(
        STEPS,
        [
            fetch_joined(mine, rows, mine_done, core),
            fetch_joined(other, rows, other_done, 1 - core),
        ],
    )
    step = pl.program_id(0)
    for part in range(0, ROWS, 32):
        span = slice(part, part + 32)
        here = rows[step, span, :].astype(F32)
        center = here - jnp.mean(here, axis=-1, keepdims=True)
        inverse = lax.rsqrt(jnp.mean(center * center, axis=-1, keepdims=True) + EPS)
        normalized = center * inverse
        normal[span, :] = normalized.astype(LOW)
        first[span, :] = (normalized * vecs[0:1, :] + vecs[1:2, :]).astype(LOW)
        second[span, :] = (normalized * vecs[2:3, :] + vecs[3:4, :]).astype(LOW)
    projected = dot(first[...], w_qkv[...], 1, 1) + b_qkv[...]
    turned = turn(projected[:, : 2 * HEAD], cosine[...], sine[...])
    here = pl.ds(pl.multiple_of(step * ROWS, ROWS), ROWS)
    queries[here, :] = turned[:, :HEAD].astype(LOW) * SCALE
    keys[here, :] = turned[:, HEAD:].astype(LOW)
    values[here, :] = projected[:, 2 * HEAD :].astype(LOW)
    for part in range(0, ROWS, 64):
        span = slice(part, part + 64)
        hidden = dot(second[span, :], w_up[...]) + b_up[...]
        share = 0.5 * (1.0 + lax.erf(hidden * (0.5**0.5)))
        active[span, :] = (hidden * share).astype(LOW)
        bell = jnp.exp(-0.5 * hidden * hidden) * ((2.0 * np.pi) ** -0.5)
        slope[span, :] = share + hidden * bell
    send_rows(active, active_send)

    place = lax.broadcasted_iota(jnp.int32, (ROWS, ROWS), 0)
    query = lax.broadcasted_iota(jnp.int32, (ROWS, ROWS), 1)
    seen = place <= query

    def block(index):
        low, high = index * ROWS, (index + 1) * ROWS
        asked = queries[low:high, :]
        near = jnp.where(seen, dot(keys[low:high, :], asked, 1, 1), -1e30)
        top = jnp.max(near, axis=0, keepdims=True)
        if index:
            far = dot(keys[:low, :], asked, 1, 1)
            top = jnp.maximum(top, jnp.max(far, axis=0, keepdims=True))
            far = jnp.exp(far - top)
        near = jnp.exp(near - top)
        total = row_sum(near)
        if index:
            total = total + row_sum(far)
        scale = 1.0 / total
        mass[0] = top + jnp.log(total)
        found = dot(values[low:high, :], (near * scale).astype(LOW), 0, 0)
        if index:
            found = found + dot(values[:low, :], (far * scale).astype(LOW), 0, 0)
        context[...] = found.T.astype(LOW)

    for index in range(STEPS):
        pl.when(step == index)(partial(block, index))
    send_rows(context, context_send)


def flat(block):
    return block.reshape(ROWS, block.shape[-1])


def mix_kernel(
    context, active, context_in, active_in, w_out, w_down, w_out_in, w_down_in, result,
    context_rows, active_rows, context_other, active_other, *done,
):
    stream(
        4,
        [
            fetch_parity(context, context_rows, done[0]),
            fetch_parity(active, active_rows, done[1]),
            fetch_double(context_in, context_other, done[2]),
            fetch_double(active_in, active_other, done[3]),
        ],
    )
    step = pl.program_id(0)
    mixed = dot(flat(context_rows[step]), w_out[...])
    mixed = mixed + dot(flat(active_rows[step]), w_down[...])
    mixed = mixed + dot(flat(context_other[step]), w_out_in[...])
    mixed = mixed + dot(flat(active_other[step]), w_down_in[...])
    result[...] = mixed.astype(LOW).reshape(2, HALF, mixed.shape[1])


def feed_back_kernel(
    mine, other, active, slope, second, context, w_down, w_out,
    grad_hidden, hidden_send, grad_context, feed_0, feed_1, feed_2, feed_3, grad_out,
    rows, active_rows, slope_rows, second_rows, up_sum, down_sum, out_sum, bias_sum, *done,
):
    step = pl.program_id(0)
    core = core_here()
    stream(
        STEPS,
        [
            fetch_joined(mine, rows, done[0], core),
            fetch_joined(other, rows, done[1], 1 - core),
            fetch_rows(active, active_rows, done[2]),
            fetch_rows(slope, slope_rows, done[3]),
            fetch_rows(second, second_rows, done[4]),
        ],
    )

    @pl.when(step == 0)
    def _():
        up_sum[...] = jnp.zeros_like(up_sum)
        down_sum[...] = jnp.zeros_like(down_sum)
        out_sum[...] = jnp.zeros_like(out_sum)
        bias_sum[...] = jnp.zeros_like(bias_sum)

    grads = rows[step]
    hidden = (dot(grads, w_down[...], 1, 1) * slope_rows[step]).astype(LOW)
    grad_hidden[...] = hidden
    send_rows(grad_hidden, hidden_send)
    grad_context[...] = dot(grads, w_out[...], 1, 1).astype(LOW)
    down_sum[...] += dot(active_rows[step], grads, 0, 0)
    out_sum[...] += dot(context[...], grads, 0, 0)
    up_sum[...] += dot(hidden, second_rows[step], 0, 0)
    bias_sum[...] += row_sum(hidden.astype(F32))

    @pl.when(step == STEPS - 1)
    def _():
        grad_out[...] = out_sum[...].astype(LOW)
        for slot, feed in enumerate((feed_0, feed_1, feed_2, feed_3)):
            span = quarter((x_here() + slot) % 4)
            feed[0:256, :] = up_sum[:, span].T.astype(LOW)
            feed[256:512, :] = down_sum[:, span].astype(LOW)
            feed[512:528, :] = jnp.broadcast_to(bias_sum[...], (16, 256)).astype(LOW)


def quarter(part):
    return pl.ds(pl.multiple_of(part * 256, 256), 256)


def attend_back_kernel(
    queries, keys, values, grad_context, mass, cosine, sine, grad_hidden, normal, w_qkv, w_up,
    own_sum, grad_projected, projected_send, sums, bias, query_sum, key_sum, value_sum,
    moments, hidden_rows, normal_rows, *done,
):
    stream(
        STEPS,
        [
            fetch_rows(grad_hidden, hidden_rows, done[0]),
            fetch_rows(normal, normal_rows, done[1]),
        ],
    )
    wide = 3 * HEAD
    place = lax.broadcasted_iota(jnp.int32, (ROWS, ROWS), 0)
    query = lax.broadcasted_iota(jnp.int32, (ROWS, ROWS), 1)
    seen = place <= query

    @pl.when(pl.program_id(0) == 0)
    def _():
        key_sum[...] = jnp.zeros_like(key_sum)
        value_sum[...] = jnp.zeros_like(value_sum)

    def block(index):
        low, high = index * ROWS, (index + 1) * ROWS
        asked = queries[low:high, :]
        grads = grad_context[...]
        spans = [slice(low, high)] + ([slice(0, low)] if index else [])
        weights, pulls = [], []
        inner = 0.0
        for number, span in enumerate(spans):
            scores = dot(keys[span, :], asked, 1, 1)
            if number == 0:
                scores = jnp.where(seen, scores, -1e30)
            weight = jnp.exp(scores - mass[0])
            pull = dot(values[span, :], grads, 1, 1)
            inner = inner + row_sum(weight * pull)
            weights.append(weight)
            pulls.append(pull)
        asked_grad = 0.0
        for span, weight, pull in zip(spans, weights, pulls):
            value_sum[span, :] += dot(weight.astype(LOW), grads)
            scores_grad = (weight * (pull - inner)).astype(LOW)
            key_sum[span, :] += dot(scores_grad, asked)
            asked_grad = asked_grad + dot(keys[span, :], scores_grad, 0, 0)
        query_sum[low:high, :] = asked_grad.T * SCALE

    for index in range(STEPS):
        pl.when(pl.program_id(0) == index)(partial(block, index))

    @pl.when(pl.program_id(0) == STEPS - 1)
    def _():
        for index in range(STEPS):
            span = slice(index * ROWS, (index + 1) * ROWS)
            both = jnp.concatenate([query_sum[span, :], key_sum[span, :]], axis=1)
            turned = turn(both, cosine[span, :], -sine[span, :])
            grad_projected[span, : 2 * HEAD] = turned.astype(LOW)
            grad_projected[span, 2 * HEAD :] = value_sum[span, :].astype(LOW)
            place = index * ROWS + (1 - core_here()) * HALF
            projected_send[index] = grad_projected[pl.ds(pl.multiple_of(place, HALF), HALF), :]
        hidden_bias, bias_here = 0.0, 0.0
        for index in range(STEPS):
            span = slice(index * ROWS, (index + 1) * ROWS)
            grads = grad_projected[span, :]
            hidden = hidden_rows[index]
            both = [dot(grads, normal_rows[index], 0, 0), dot(hidden, normal_rows[index], 0, 0)]
            if index:
                moments[0:wide, :] += both[0]
                moments[wide:, :] += both[1]
            else:
                moments[0:wide, :] = both[0]
                moments[wide:, :] = both[1]
            bias_here = bias_here + row_sum(grads.astype(F32))
            hidden_bias = hidden_bias + row_sum(hidden.astype(F32))
        bias[...] = bias_here
        sums[0:1, :] = row_sum(moments[0:wide, :] * w_qkv[...].astype(F32))
        sums[1:2, :] = dot_full(bias_here, w_qkv[...], 0)
        sums[2:3, :] = row_sum(moments[wide:, :] * w_up[...].astype(F32).T)
        sums[3:4, :] = dot_full(hidden_bias, w_up[...], 1)
        sums[4:5, :] = own_sum[...]


def input_back_kernel(
    projected, hidden, projected_in, hidden_in, vecs, w_qkv, w_up, w_qkv_in, w_up_in, sums,
    result, projected_rows, hidden_rows, projected_other, hidden_other, *done,
):
    stream(
        4,
        [
            fetch_parity(projected, projected_rows, done[0]),
            fetch_parity(hidden, hidden_rows, done[1]),
            fetch_double(projected_in, projected_other, done[2]),
            fetch_double(hidden_in, hidden_other, done[3]),
        ],
    )
    step = pl.program_id(0)
    one = dot(flat(projected_rows[step]), w_qkv[...])
    one = one + dot(flat(projected_other[step]), w_qkv_in[...])
    two = dot(flat(hidden_rows[step]), w_up[...], 1, 1)
    two = two + dot(flat(hidden_other[step]), w_up_in[...], 1, 1)
    weighted = one * vecs[0:1, :] + two * vecs[2:3, :]
    result[:, 0:HALF, :] = weighted.astype(LOW).reshape(2, HALF, weighted.shape[1])
    high = sums[...].astype(LOW).astype(F32)
    rest = jnp.zeros((EXTRA - 10, weighted.shape[1]), F32)
    tail = jnp.concatenate([high, sums[...] - high, rest], axis=0).astype(LOW)
    result[0, HALF:, :] = tail
    result[1, HALF:, :] = tail


def dot_full(left, right, right_axis):
    return lax.dot_general(
        left,
        right.astype(F32),
        (((1,), (right_axis,)), ((), ())),
        precision=lax.Precision.HIGHEST,
        preferred_element_type=F32,
    )


def qkv_grad_kernel(
    grad_projected, first, grad_out, bias, head_0, head_1, head_2, head_3, qkv_sum,
    first_rows, done,
):
    step = pl.program_id(0)
    wide = 3 * HEAD
    stream(STEPS, [fetch_rows(first, first_rows, done)])

    @pl.when(step == 0)
    def _():
        qkv_sum[...] = jnp.zeros_like(qkv_sum)

    qkv_sum[...] += dot(grad_projected[...], first_rows[step], 0, 0)

    @pl.when(step == STEPS - 1)
    def _():
        for slot, head in enumerate((head_0, head_1, head_2, head_3)):
            span = quarter((x_here() + slot) % 4)
            head[0:wide, :] = qkv_sum[:, span].astype(LOW)
            head[wide:256, :] = grad_out[:, span]
            head[256:272, :wide] = jnp.broadcast_to(bias[...], (16, wide)).astype(LOW)
            head[256:272, wide:] = jnp.zeros((16, 256 - wide), LOW)


def small_kernel(parts, sums):
    tail = jnp.sum(parts[...].astype(F32), axis=0)
    sums[...] = tail[0:5] + tail[5:10]


def finish_grads_kernel(
    feed_0, feed_1, feed_2, feed_3, head_0, head_1, head_2, head_3,
    grad_qkv, grad_qkv_bias, grad_out, grad_up, grad_up_bias, grad_down,
):
    wide = 3 * HEAD
    for slot, feed in enumerate((feed_0, feed_1, feed_2, feed_3)):
        span = quarter((x_here() + 4 - slot) % 4)
        grad_up[span, :] = feed[0:256, :].astype(F32)
        grad_down[:, span] = feed[256:512, :].astype(F32)
    for slot, head in enumerate((head_0, head_1, head_2, head_3)):
        span = quarter((x_here() + 4 - slot) % 4)
        grad_qkv[:, span] = head[0:wide, :].astype(F32)
        grad_out[:, span] = head[wide:256, :].astype(F32)
    grad_up_bias[...] = feed_0[512:513, :].astype(F32)
    grad_qkv_bias[...] = head_0[256:257, :wide].astype(F32)


def finish_out_kernel(parts, tokens, out_bias, layer_out):
    total = jnp.sum(parts[...].astype(F32), axis=0)
    layer_out[...] = (tokens[...].astype(F32) + total + out_bias[...].astype(F32)).astype(LOW)


def finish_back_kernel(parts, tokens, cotangent, input_grad):
    scaled = jnp.sum(parts[:, 0:HALF, :].astype(F32), axis=0)
    normalized, inverse = normalize(tokens[...].astype(F32))
    input_grad[...] = (
        cotangent[...].astype(F32) + norm_back(scaled, normalized, inverse)
    ).astype(LOW)


def arrivals(count):
    return pltpu.SemaphoreType.DMA((count,))


def whole(shape):
    return pl.BlockSpec(shape, lambda step: (0,) * len(shape))


def by_rows(columns):
    return pl.BlockSpec((ROWS, columns), lambda step: (step, 0))


LEFT = pl.BlockSpec(memory_space=pltpu.HBM)
MASS = pl.BlockSpec((1, 1, ROWS), lambda step: (step, 0, 0))


def shape(dims, kind):
    return jax.ShapeDtypeStruct(dims, kind)


COST = pl.CostEstimate(flops=1, bytes_accessed=1, transcendentals=0)


def left(dims, kind):
    return pltpu.HBM(dims, kind)


def launch(kernel, name, ins, outs, out_shapes, scratch, steps=STEPS, room=60):
    return pl.pallas_call(
        kernel,
        name=name,
        grid=(steps,),
        in_specs=ins,
        out_specs=outs,
        scratch_shapes=scratch,
        out_shape=out_shapes,
        compiler_params=pltpu.CompilerParams(vmem_limit_bytes=room * 2**20),
        cost_estimate=COST,
    )


def half_rows(columns):
    return pl.BlockSpec((1, HALF, columns), lambda step: (step, 0, 0))


def four(value):
    return value.reshape(STEPS, 2, HALF, value.shape[1])


def per_device(
    tokens, w_qkv, b_qkv, w_out, w_up, b_up, w_down, out_bias,
    ln1_gain, ln1_shift, ln2_gain, ln2_shift, cotangent,
):
    model = w_up.shape[0]
    feed_here = w_up.shape[1]
    wide = 3 * HEAD
    w_qkv = w_qkv.transpose(1, 2, 0).reshape(wide, model)
    w_out = w_out.reshape(HEAD, model)
    vecs = jnp.stack([ln1_gain, ln1_shift, ln2_gain, ln2_shift]).astype(F32)
    cosine, sine = rotary_tables()
    own_sum = jnp.sum(cotangent.astype(F32), axis=0)[None, :]

    held = copies(cotangent, 8)
    mine = trade_chips(copies(tokens, 8))
    weights_in = [swap_core(w) for w in (w_out, w_down, w_qkv, w_up)]
    held, vecs, b_qkv, b_up, own_sum, mine, *weights_in = lax.optimization_barrier(
        (held, vecs, b_qkv.astype(F32), b_up.astype(F32)[None, :], own_sum, mine)
        + tuple(weights_in)
    )
    w_out_in, w_down_in, w_qkv_in, w_up_in = weights_in
    other = swap_core(mine)
    grad_mine = trade_chips(held)

    halves = shape((STEPS, HALF, feed_here), LOW)
    (
        first, second, normal, queries, keys, values, active, active_send, slope,
        context, context_send, mass,
    ) = launch(
        forward_kernel,
        "forward",
        [
            LEFT, LEFT, whole((4, model)), whole((wide, model)), whole((1, wide)),
            whole((model, feed_here)), whole((1, feed_here)), by_rows(128), by_rows(128),
        ],
        [
            by_rows(model), by_rows(model), by_rows(model), whole((LEN, HEAD)),
            whole((LEN, HEAD)), whole((LEN, HEAD)), by_rows(feed_here), half_rows(feed_here),
            by_rows(feed_here), by_rows(HEAD), half_rows(HEAD), MASS,
        ],
        [
            left((LEN, model), LOW), left((LEN, model), LOW), left((LEN, model), LOW),
            shape((LEN, HEAD), LOW), shape((LEN, HEAD), LOW), shape((LEN, HEAD), LOW),
            left((LEN, feed_here), LOW), halves, left((LEN, feed_here), F32),
            shape((LEN, HEAD), LOW), shape((STEPS, HALF, HEAD), LOW),
            shape((STEPS, 1, ROWS), F32),
        ],
        [pltpu.VMEM((STEPS, ROWS, model), LOW), arrivals(STEPS), arrivals(STEPS)],
    )(mine, other, vecs, w_qkv, b_qkv, w_up, b_up, cosine, sine)
    active_in = swap_core(active_send)
    context_in = swap_core(context_send)

    mixed = launch(
        mix_kernel,
        "mix",
        [LEFT] * 4 + [whole((HEAD, model)), whole((feed_here, model))] * 2,
        pl.BlockSpec((2, HALF, model), lambda step: (step, 0, 0)),
        left((STEPS, HALF, model), LOW),
        [pltpu.VMEM((4, 2, HALF, HEAD), LOW), pltpu.VMEM((4, 2, HALF, feed_here), LOW)] * 2
        + [arrivals(4)] * 4,
        steps=4,
    )(four(context), four(active), context_in, active_in, w_out, w_down, w_out_in, w_down_in)

    grad_mine, mixed = lax.optimization_barrier((grad_mine, mixed))
    grad_other = swap_core(grad_mine)
    branch = trade_chips(mixed)

    grad_hidden, hidden_send, grad_context, *feed, grad_out = launch(
        feed_back_kernel,
        "feed_back",
        [
            LEFT, LEFT, LEFT, LEFT, LEFT,
            by_rows(HEAD), whole((feed_here, model)), whole((HEAD, model)),
        ],
        [by_rows(feed_here), half_rows(feed_here), by_rows(HEAD)]
        + [whole((528, 256))] * 4 + [whole((HEAD, model))],
        [shape((LEN, feed_here), LOW), halves, shape((LEN, HEAD), LOW)]
        + [shape((528, 256), LOW)] * 4 + [shape((HEAD, model), LOW)],
        [
            pltpu.VMEM((STEPS, ROWS, model), LOW), pltpu.VMEM((STEPS, ROWS, feed_here), LOW),
            pltpu.VMEM((STEPS, ROWS, feed_here), F32), pltpu.VMEM((STEPS, ROWS, model), LOW),
            pltpu.VMEM((feed_here, model), F32), pltpu.VMEM((feed_here, model), F32),
            pltpu.VMEM((HEAD, model), F32), pltpu.VMEM((1, feed_here), F32),
        ]
        + [arrivals(STEPS)] * 5,
    )(grad_mine, grad_other, active, slope, second, context, w_down, w_out)
    hidden_in = swap_core(hidden_send)
    feed_moved = [move_x(feed[distance], distance) for distance in range(1, 4)]

    grad_projected, projected_send, sums, bias = launch(
        attend_back_kernel,
        "attend_back",
        [
            whole((LEN, HEAD)), whole((LEN, HEAD)), whole((LEN, HEAD)), by_rows(HEAD), MASS,
            whole((LEN, 128)), whole((LEN, 128)), LEFT, LEFT, whole((wide, model)),
            whole((model, feed_here)), whole((1, model)),
        ],
        [whole((LEN, wide)), whole((STEPS, HALF, wide)), whole((5, model)), whole((1, wide))],
        [
            shape((LEN, wide), LOW), shape((STEPS, HALF, wide), LOW), shape((5, model), F32),
            shape((1, wide), F32),
        ],
        [pltpu.VMEM((LEN, HEAD), F32)] * 3
        + [
            pltpu.VMEM((wide + feed_here, model), F32),
            pltpu.VMEM((STEPS, ROWS, feed_here), LOW), pltpu.VMEM((STEPS, ROWS, model), LOW),
        ]
        + [arrivals(STEPS)] * 2,
    )(
        queries, keys, values, grad_context, mass, cosine, sine, grad_hidden, normal,
        w_qkv, w_up, own_sum,
    )
    sums = sums + swap_core(sums)
    grad_projected, projected_send, branch, hidden_in, *feed_moved = lax.optimization_barrier(
        (grad_projected, projected_send, branch, hidden_in, *feed_moved)
    )
    projected_in = swap_core(projected_send)
    feed_half = add_four(feed[0], feed_moved)
    feed_other = lax.ppermute(feed_half, "dp", Z_PAIR)

    both = launch(
        input_back_kernel,
        "input_back",
        [LEFT] * 4 + [whole((4, model))] + [whole((wide, model)), whole((model, feed_here))] * 2
        + [whole((5, model))],
        pl.BlockSpec((2, HALF + EXTRA, model), lambda step: (step, 0, 0)),
        left((STEPS, HALF + EXTRA, model), LOW),
        [pltpu.VMEM((4, 2, HALF, wide), LOW), pltpu.VMEM((4, 2, HALF, feed_here), LOW)] * 2
        + [arrivals(4)] * 4,
        steps=4,
    )(
        four(grad_projected), four(grad_hidden), projected_in, hidden_in, vecs,
        w_qkv, w_up, w_qkv_in, w_up_in, sums,
    )
    both, grad_projected, feed_other = lax.optimization_barrier(
        (both, grad_projected, feed_other)
    )
    feed_low = add_low(feed_half, feed_other)
    scaled = trade_chips(both)
    head = launch(
        qkv_grad_kernel,
        "qkv_grad",
        [by_rows(wide), LEFT, whole((HEAD, model)), whole((1, wide))],
        [whole((272, 256))] * 4,
        [shape((272, 256), LOW)] * 4,
        [
            pltpu.VMEM((wide, model), F32), pltpu.VMEM((STEPS, ROWS, model), LOW),
            arrivals(STEPS),
        ],
        room=40,
    )(grad_projected, first, grad_out, bias)
    head_moved = [move_x(head[distance], distance) for distance in range(1, 4)]
    head_low = sum_z(add_four(head[0], head_moved))
    feed_parts = spread_x(feed_low)
    head_parts = spread_x(head_low)

    layer_out = pl.pallas_call(
        finish_out_kernel,
        name="finish_out",
        out_shape=shape(tokens.shape, LOW),
        cost_estimate=COST,
    )(branch, tokens, out_bias[None, :])
    scaled, layer_out, *parts = lax.optimization_barrier(
        (scaled, layer_out, *feed_parts, *head_parts)
    )
    small = pl.pallas_call(
        small_kernel,
        name="small",
        grid=(1,),
        in_specs=[pl.BlockSpec((STEPS, EXTRA, model), lambda step: (0, HALF // EXTRA, 0))],
        out_specs=whole((5, model)),
        out_shape=shape((5, model), F32),
        cost_estimate=COST,
    )(scaled)
    small_moved = lax.ppermute(small, "dp", Z_PAIR)
    input_grad = pl.pallas_call(
        finish_back_kernel,
        name="finish_back",
        grid=(1,),
        in_specs=[
            whole((STEPS, HALF, model)), whole(tokens.shape), whole(tokens.shape),
        ],
        out_specs=whole(tokens.shape),
        out_shape=shape(tokens.shape, LOW),
        cost_estimate=COST,
    )(scaled, tokens, cotangent)
    small_moved, input_grad = lax.optimization_barrier((small_moved, input_grad))
    grad_qkv, grad_qkv_bias, grad_out, grad_up, grad_up_bias, grad_down = pl.pallas_call(
        finish_grads_kernel,
        name="finish_grads",
        out_shape=[
            shape((wide, model), F32), shape((1, wide), F32), shape((HEAD, model), F32),
            shape((model, feed_here), F32), shape((1, feed_here), F32),
            shape((feed_here, model), F32),
        ],
        cost_estimate=COST,
    )(*parts)
    small = sum_four(small + small_moved, move_x)

    return (
        layer_out,
        input_grad,
        grad_qkv.reshape(1, wide, model).transpose(2, 0, 1),
        grad_qkv_bias,
        grad_out.reshape(1, HEAD, model),
        grad_up,
        grad_up_bias[0],
        grad_down,
        small[4],
        small[0],
        small[1],
        small[2],
        small[3],
    )


def solution(mesh):
    placed = (
        P(("dp", "tensor"), None),
        P(None, "tensor", None),
        P("tensor", None),
        P("tensor", None, None),
        P(None, "tensor"),
        P("tensor"),
        P("tensor", None),
        P(),
        P(),
        P(),
        P(),
        P(),
        P(("dp", "tensor"), None),
    )
    return jax.shard_map(
        per_device,
        mesh=mesh,
        in_specs=placed,
        out_specs=(
            P(("dp", "tensor"), None),
            P(("dp", "tensor"), None),
            P(None, "tensor", None),
            P("tensor", None),
            P("tensor", None, None),
            P(None, "tensor"),
            P("tensor"),
            P("tensor", None),
            P(),
            P(),
            P(),
            P(),
            P(),
        ),
        check_vma=False,
    )
```

```python
from functools import partial

import jax
import jax.numpy as jnp
import numpy as np
from jax import lax
from jax.experimental import pallas as pl
from jax.experimental.pallas import tpu as pltpu
from jax.sharding import PartitionSpec as P

ROT = 16
LEN = 2048
EPS = 1e-05
HEAD = 64
ROWS = 256
STEPS = LEN // ROWS
HALF = ROWS // 2
SCALE = HEAD ** (-0.5)

SAME_CORE = [[c + 2 * i for i in range(8)] for c in range(2)]
SAME_Y = [[c + 4 * i for i in range(4)] for c in range(4)]
PAIR = [(i, i ^ 1) for i in range(16)]
Z_NEAR = [(i, i ^ 2) for i in range(16)]
Z_PAIR = [(i, i ^ 1) for i in range(8)]

F32 = jnp.float32
LOW = jnp.bfloat16


def swap_core(value):
    return lax.ppermute(value, "tensor", PAIR)


def trade_chips(blocks):
    return lax.all_to_all(blocks, "tensor", 0, 0, axis_index_groups=SAME_CORE, tiled=True)


def trade_y(blocks):
    return lax.all_to_all(blocks, "tensor", 0, 0, axis_index_groups=SAME_Y, tiled=True)


def copies(block, count):
    return jnp.broadcast_to(block[None], (count,) + block.shape)


def move_x(value, distance):
    pairs = [(i, (i // 2 + distance) % 4 * 2 + i % 2) for i in range(8)]
    return lax.ppermute(value, "dp", pairs)


def add_four(own, moved):
    total = own.astype(F32)
    for part in moved:
        total = total + part.astype(F32)
    return total.astype(LOW)


def add_low(left, right):
    return (left.astype(F32) + right.astype(F32)).astype(LOW)


def sum_four(rows, move):
    return (rows + move(rows, 2)) + (move(rows, 1) + move(rows, 3))


def move_y(value, distance):
    pairs = [(i, (i // 4 + distance) % 4 * 4 + i % 4) for i in range(16)]
    return lax.ppermute(value, "tensor", pairs)


def spread_x(low):
    return [low] + [move_x(low, distance) for distance in range(1, 4)]


def normalize(values):
    center = values - jnp.mean(values, axis=-1, keepdims=True)
    inverse = lax.rsqrt(jnp.mean(center * center, axis=-1, keepdims=True) + EPS)
    return (center * inverse, inverse)


def norm_back(scaled, normalized, inverse):
    centered = scaled - jnp.mean(scaled, axis=-1, keepdims=True)
    return inverse * (centered - normalized * jnp.mean(scaled * normalized, axis=-1, keepdims=True))


def rotary_tables():
    lane = np.arange(2 * HEAD) % HEAD
    half = ROT // 2
    inverse = np.float32(10000.0) ** (-2.0 * (lane % half).astype(np.float32) / np.float32(ROT))
    inverse = np.where(lane < ROT, inverse, 0.0).astype(np.float32)
    angles = np.arange(LEN, dtype=np.float32)[:, None] * inverse[None, :]
    sign = np.where(lane < half, -1.0, 1.0).astype(np.float32)
    return np.cos(angles).astype(np.float32), (np.sin(angles) * sign).astype(np.float32)


def turn(values, cosine, sine):
    lane = lax.broadcasted_iota(jnp.int32, values.shape, 1) % HEAD
    partner = jnp.where(
        lane < ROT // 2,
        pltpu.roll(values, 2 * HEAD - ROT // 2, 1),
        pltpu.roll(values, ROT // 2, 1),
    )
    return values * cosine + partner * sine


def dot(left, right, left_axis=1, right_axis=0):
    return lax.dot_general(
        left,
        right,
        (((left_axis,), (right_axis,)), ((), ())),
        preferred_element_type=F32,
    )


def core_here():
    return lax.axis_index("tensor") % 2


def stream(steps, each, moves):
    step = pl.program_id(0)

    @pl.when(step == 0)
    def _():
        for place in range(steps // each):
            for move in moves:
                move(place).start()

    @pl.when(step % each == 0)
    def _():
        for move in moves:
            move(step // each).wait()


def fetch(source, target, done):
    def move(place):
        return pltpu.make_async_copy(source(place), target(place), done.at[place])

    return move


def fetch_rows(source, target, done, each):
    return fetch(
        lambda place: source.at[pl.ds(place * each, each)],
        lambda place: target.at[pl.ds(place * each, each)],
        done,
    )


def fetch_parity(source, target, done, each):
    core = core_here()
    return fetch(
        lambda place: source.at[pl.ds(place * each, each), core],
        lambda place: target.at[pl.ds(place * each, each)],
        done,
    )


def fetch_joined(source, target, done, each, core):
    start = pl.multiple_of(core * HALF, HALF)
    return fetch(
        lambda place: source.at[pl.ds(place * each, each)],
        lambda place: target.at[pl.ds(place * each, each), pl.ds(start, HALF)],
        done,
    )


def send_rows(block, send):
    core = core_here()
    send[0] = block[pl.ds(pl.multiple_of((1 - core) * HALF, HALF), HALF), :]


def x_here():
    return lax.axis_index("dp") // 2


def renormalize(rows, stats):
    return (rows.astype(F32) - stats[:, 0:1]) * stats[:, 1:2]


def row_sum(values):
    return jnp.sum(values, axis=0, keepdims=True)


def forward_kernel(
    mine, other, vecs, w_qkv, b_qkv, w_up, b_up, cosine, sine,
    stats, queries, keys, values, active, active_send, slope,
    context, context_send, mass, rows, first, second, mine_done, other_done,
):
    core = core_here()
    stream(
        STEPS,
        2,
        [
            fetch_joined(mine, rows, mine_done, 2, core),
            fetch_joined(other, rows, other_done, 2, 1 - core),
        ],
    )
    step = pl.program_id(0)
    for part in range(0, ROWS, 32):
        span = slice(part, part + 32)
        here = rows[step, span, :].astype(F32)
        mean = jnp.mean(here, axis=-1, keepdims=True)
        center = here - mean
        inverse = lax.rsqrt(jnp.mean(center * center, axis=-1, keepdims=True) + EPS)
        normalized = center * inverse
        lane = lax.broadcasted_iota(jnp.int32, (32, 128), 1)
        stats[span, :] = jnp.where(lane == 0, mean, inverse)
        first[span, :] = (normalized * vecs[0:1, :] + vecs[1:2, :]).astype(LOW)
        second[span, :] = (normalized * vecs[2:3, :] + vecs[3:4, :]).astype(LOW)
    projected = dot(first[...], w_qkv[...], 1, 1) + b_qkv[...]
    turned = turn(projected[:, : 2 * HEAD], cosine[...], sine[...])
    here = pl.ds(pl.multiple_of(step * ROWS, ROWS), ROWS)
    queries[here, :] = turned[:, :HEAD].astype(LOW) * SCALE
    keys[here, :] = turned[:, HEAD:].astype(LOW)
    values[here, :] = projected[:, 2 * HEAD :].astype(LOW)
    for part in range(0, ROWS, 64):
        span = slice(part, part + 64)
        hidden = dot(second[span, :], w_up[...]) + b_up[...]
        share = 0.5 * (1.0 + lax.erf(hidden * (0.5**0.5)))
        active[span, :] = (hidden * share).astype(LOW)
        bell = jnp.exp(-0.5 * hidden * hidden) * ((2.0 * np.pi) ** -0.5)
        slope[span, :] = share + hidden * bell
    send_rows(active, active_send)

    place = lax.broadcasted_iota(jnp.int32, (ROWS, ROWS), 0)
    query = lax.broadcasted_iota(jnp.int32, (ROWS, ROWS), 1)
    seen = place <= query

    def block(index):
        low, high = index * ROWS, (index + 1) * ROWS
        asked = queries[low:high, :]
        near = jnp.where(seen, dot(keys[low:high, :], asked, 1, 1), -1e30)
        top = jnp.max(near, axis=0, keepdims=True)
        if index:
            far = dot(keys[:low, :], asked, 1, 1)
            top = jnp.maximum(top, jnp.max(far, axis=0, keepdims=True))
            far = jnp.exp(far - top)
        near = jnp.exp(near - top)
        total = row_sum(near)
        if index:
            total = total + row_sum(far)
        scale = 1.0 / total
        mass[0] = top + jnp.log(total)
        found = dot(values[low:high, :], (near * scale).astype(LOW), 0, 0)
        if index:
            found = found + dot(values[:low, :], (far * scale).astype(LOW), 0, 0)
        context[...] = found.T.astype(LOW)

    for index in range(STEPS):
        pl.when(step == index)(partial(block, index))
    send_rows(context, context_send)


def flat(block):
    return block.reshape(ROWS, block.shape[-1])


def mix_kernel(
    context, active, context_in, active_in, w_out, w_down, w_out_in, w_down_in, result,
    context_rows, active_rows, context_other, active_other, *done,
):
    stream(
        STEPS // 2,
        STEPS // 2,
        [
            fetch_parity(context, context_rows, done[0], STEPS),
            fetch_parity(active, active_rows, done[1], STEPS),
            fetch_rows(context_in, context_other, done[2], STEPS),
            fetch_rows(active_in, active_other, done[3], STEPS),
        ],
    )
    here = pl.ds(pl.program_id(0) * 2, 2)
    mixed = dot(flat(context_rows[here]), w_out[...])
    mixed = mixed + dot(flat(active_rows[here]), w_down[...])
    mixed = mixed + dot(flat(context_other[here]), w_out_in[...])
    mixed = mixed + dot(flat(active_other[here]), w_down_in[...])
    result[...] = mixed.astype(LOW).reshape(2, HALF, mixed.shape[1])


def feed_back_kernel(
    mine, other, active, slope, tokens_mine, tokens_other, stats, vecs, context, w_down, w_out,
    grad_hidden, hidden_send, grad_context, feed_0, feed_1, feed_2, feed_3, grad_out,
    rows, active_rows, slope_rows, token_rows, stats_rows, second, up_sum, down_sum, out_sum,
    bias_sum, *done,
):
    step = pl.program_id(0)
    core = core_here()
    stream(
        STEPS,
        2,
        [
            fetch_joined(mine, rows, done[0], 2, core),
            fetch_joined(other, rows, done[1], 2, 1 - core),
            fetch_rows(active, active_rows, done[2], 2),
            fetch_rows(slope, slope_rows, done[3], 2),
            fetch_rows(stats, stats_rows, done[4], 2),
            fetch_joined(tokens_mine, token_rows, done[5], 2, core),
            fetch_joined(tokens_other, token_rows, done[6], 2, 1 - core),
        ],
    )

    @pl.when(step == 0)
    def _():
        up_sum[...] = jnp.zeros_like(up_sum)
        down_sum[...] = jnp.zeros_like(down_sum)
        out_sum[...] = jnp.zeros_like(out_sum)
        bias_sum[...] = jnp.zeros_like(bias_sum)

    grads = rows[step]
    hidden = (dot(grads, w_down[...], 1, 1) * slope_rows[step]).astype(LOW)
    grad_hidden[...] = hidden
    send_rows(grad_hidden, hidden_send)
    grad_context[...] = dot(grads, w_out[...], 1, 1).astype(LOW)
    down_sum[...] += dot(active_rows[step], grads, 0, 0)
    out_sum[...] += dot(context[...], grads, 0, 0)
    for part in range(0, ROWS, 32):
        span = slice(part, part + 32)
        normalized = renormalize(token_rows[step, span, :], stats_rows[step, span, :])
        second[span, :] = (normalized * vecs[2:3, :] + vecs[3:4, :]).astype(LOW)
    up_sum[...] += dot(hidden, second[...], 0, 0)
    bias_sum[...] += row_sum(hidden.astype(F32))

    @pl.when(step == STEPS - 1)
    def _():
        grad_out[...] = out_sum[...].astype(LOW)
        for slot, feed in enumerate((feed_0, feed_1, feed_2, feed_3)):
            span = quarter((x_here() + slot) % 4)
            feed[0:256, :] = up_sum[:, span].T.astype(LOW)
            feed[256:512, :] = down_sum[:, span].astype(LOW)
            feed[512:528, :] = jnp.broadcast_to(bias_sum[...], (16, 256)).astype(LOW)


def quarter(part):
    return pl.ds(pl.multiple_of(part * 256, 256), 256)


def attend_back_kernel(
    queries, keys, values, grad_context, mass, cosine, sine, grad_hidden, stats, mine, other,
    w_qkv, w_up, vecs, own_sum, grad_out,
    grad_projected, projected_send, head_0, head_1, head_2, head_3, sums,
    query_sum, key_sum, value_sum, qkv_sum, moments, first, normal,
    cosine_rows, sine_rows, hidden_rows, stats_rows, token_rows, qkv_rows, up_rows, *done,
):
    wide = 3 * HEAD

    def later():
        pairs = [
            (cosine, cosine_rows), (sine, sine_rows), (grad_hidden, hidden_rows),
            (stats, stats_rows), (w_qkv, qkv_rows), (w_up, up_rows),
        ]
        for source, core in ((mine, core_here()), (other, 1 - core_here())):
            start = pl.multiple_of(core * HALF, HALF)
            pairs.append((source, token_rows.at[:, pl.ds(start, HALF)]))
        return [pltpu.make_async_copy(*pair, mark) for pair, mark in zip(pairs, done)]

    @pl.when(pl.program_id(0) == 0)
    def _():
        for copy in later():
            copy.start()

    place = lax.broadcasted_iota(jnp.int32, (ROWS, ROWS), 0)
    query = lax.broadcasted_iota(jnp.int32, (ROWS, ROWS), 1)
    seen = place <= query

    @pl.when(pl.program_id(0) == 0)
    def _():
        key_sum[...] = jnp.zeros_like(key_sum)
        value_sum[...] = jnp.zeros_like(value_sum)

    def block(index):
        low, high = index * ROWS, (index + 1) * ROWS
        asked = queries[low:high, :]
        grads = grad_context[...]
        spans = [slice(low, high)] + ([slice(0, low)] if index else [])
        weights, pulls = [], []
        inner = 0.0
        for number, span in enumerate(spans):
            scores = dot(keys[span, :], asked, 1, 1)
            if number == 0:
                scores = jnp.where(seen, scores, -1e30)
            weight = jnp.exp(scores - mass[0])
            pull = dot(values[span, :], grads, 1, 1)
            inner = inner + row_sum(weight * pull)
            weights.append(weight)
            pulls.append(pull)
        asked_grad = 0.0
        for span, weight, pull in zip(spans, weights, pulls):
            value_sum[span, :] += dot(weight.astype(LOW), grads)
            scores_grad = (weight * (pull - inner)).astype(LOW)
            key_sum[span, :] += dot(scores_grad, asked)
            asked_grad = asked_grad + dot(keys[span, :], scores_grad, 0, 0)
        query_sum[low:high, :] = asked_grad.T * SCALE

    for index in range(STEPS):
        pl.when(pl.program_id(0) == index)(partial(block, index))

    @pl.when(pl.program_id(0) == STEPS - 1)
    def _():
        for copy in later():
            copy.wait()
        for index in range(STEPS):
            span = slice(index * ROWS, (index + 1) * ROWS)
            both = jnp.concatenate([query_sum[span, :], key_sum[span, :]], axis=1)
            turned = turn(both, cosine_rows[span, :], -sine_rows[span, :])
            grad_projected[span, : 2 * HEAD] = turned.astype(LOW)
            grad_projected[span, 2 * HEAD :] = value_sum[span, :].astype(LOW)
            place = index * ROWS + (1 - core_here()) * HALF
            projected_send[index] = grad_projected[pl.ds(pl.multiple_of(place, HALF), HALF), :]
        hidden_bias, bias = 0.0, 0.0
        for index in range(STEPS):
            span = slice(index * ROWS, (index + 1) * ROWS)
            for part in range(0, ROWS, 32):
                rows = slice(part, part + 32)
                place = slice(index * ROWS + part, index * ROWS + part + 32)
                normalized = renormalize(token_rows[index, rows, :], stats_rows[place, :])
                normal[rows, :] = normalized.astype(LOW)
                first[rows, :] = (normalized * vecs[0:1, :] + vecs[1:2, :]).astype(LOW)
            grads = grad_projected[span, :]
            hidden = hidden_rows[span, :]
            here = normal[...]
            added = dot(grads, first[...], 0, 0), dot(grads, here, 0, 0), dot(hidden, here, 0, 0)
            if index:
                qkv_sum[...] += added[0]
                moments[0:wide, :] += added[1]
                moments[wide:, :] += added[2]
            else:
                qkv_sum[...] = added[0]
                moments[0:wide, :] = added[1]
                moments[wide:, :] = added[2]
            bias = bias + row_sum(grads.astype(F32))
            hidden_bias = hidden_bias + row_sum(hidden.astype(F32))
        for slot, head in enumerate((head_0, head_1, head_2, head_3)):
            span = quarter((x_here() + slot) % 4)
            head[0:wide, :] = qkv_sum[:, span].astype(LOW)
            head[wide:256, :] = grad_out[:, span]
            head[256:272, :wide] = jnp.broadcast_to(bias, (16, wide)).astype(LOW)
            head[256:272, wide:] = jnp.zeros((16, 256 - wide), LOW)
        sums[0:1, :] = row_sum(moments[0:wide, :] * qkv_rows[...].astype(F32))
        sums[1:2, :] = dot_full(bias, qkv_rows[...], 0)
        sums[2:3, :] = row_sum(moments[wide:, :] * up_rows[...].astype(F32).T)
        sums[3:4, :] = dot_full(hidden_bias, up_rows[...], 1)
        sums[4:5, :] = own_sum[...]


def input_back_kernel(
    projected, hidden, projected_in, hidden_in, vecs, w_qkv, w_up, w_qkv_in, w_up_in,
    result, projected_rows, hidden_rows, projected_other, hidden_other, *done,
):
    stream(
        STEPS // 2,
        STEPS // 2,
        [
            fetch_parity(projected, projected_rows, done[0], STEPS),
            fetch_parity(hidden, hidden_rows, done[1], STEPS),
            fetch_rows(projected_in, projected_other, done[2], STEPS),
            fetch_rows(hidden_in, hidden_other, done[3], STEPS),
        ],
    )
    here = pl.ds(pl.program_id(0) * 2, 2)
    one = dot(flat(projected_rows[here]), w_qkv[...])
    one = one + dot(flat(projected_other[here]), w_qkv_in[...])
    two = dot(flat(hidden_rows[here]), w_up[...], 1, 1)
    two = two + dot(flat(hidden_other[here]), w_up_in[...], 1, 1)
    weighted = one * vecs[0:1, :] + two * vecs[2:3, :]
    result[...] = weighted.astype(LOW).reshape(2, HALF, weighted.shape[1])


def dot_full(left, right, right_axis):
    return lax.dot_general(
        left,
        right.astype(F32),
        (((1,), (right_axis,)), ((), ())),
        precision=lax.Precision.HIGHEST,
        preferred_element_type=F32,
    )


def fold_kernel(parts, keep, send):
    own = lax.axis_index("tensor") // 2 % 2

    def total(start):
        span = pl.ds(pl.multiple_of(start, HALF), HALF)
        result = parts[0, span, :].astype(F32)
        for number in range(1, 4):
            result = result + parts[number, span, :].astype(F32)
        return result

    keep[...] = total(own * HALF)
    send[...] = total((1 - own) * HALF).astype(LOW)


def finish_grads_kernel(
    part_0, part_1, part_2, part_3,
    grad_qkv, grad_qkv_bias, grad_out, grad_up, grad_up_bias, grad_down,
):
    wide = 3 * HEAD
    for slot, part in enumerate((part_0, part_1, part_2, part_3)):
        span = quarter((x_here() + 4 - slot) % 4)
        grad_up[span, :] = part[0:256, :].astype(F32)
        grad_down[:, span] = part[256:512, :].astype(F32)
        grad_qkv[:, span] = part[528 : 528 + wide, :].astype(F32)
        grad_out[:, span] = part[528 + wide : 784, :].astype(F32)
    grad_up_bias[...] = part_0[512:513, :].astype(F32)
    grad_qkv_bias[...] = part_0[784:785, :wide].astype(F32)


def finish_out_kernel(parts, tokens, out_bias, layer_out):
    total = jnp.sum(parts[...].astype(F32), axis=0)
    layer_out[...] = (tokens[...].astype(F32) + total + out_bias[...].astype(F32)).astype(LOW)


def finish_back_kernel(keep, part, tokens, cotangent, input_grad):
    scaled = keep[...] + part[...].astype(F32)
    normalized, inverse = normalize(tokens[...].astype(F32))
    input_grad[...] = (
        cotangent[...].astype(F32) + norm_back(scaled, normalized, inverse)
    ).astype(LOW)


def arrivals(count):
    return pltpu.SemaphoreType.DMA((count,))


def whole(shape):
    return pl.BlockSpec(shape, lambda step: (0,) * len(shape))


def by_rows(columns):
    return pl.BlockSpec((ROWS, columns), lambda step: (step, 0))


LEFT = pl.BlockSpec(memory_space=pltpu.HBM)
MASS = pl.BlockSpec((1, 1, ROWS), lambda step: (step, 0, 0))


def shape(dims, kind):
    return jax.ShapeDtypeStruct(dims, kind)


COST = pl.CostEstimate(flops=1, bytes_accessed=1, transcendentals=0)


def left(dims, kind):
    return pltpu.HBM(dims, kind)


def launch(kernel, name, ins, outs, out_shapes, scratch, steps=STEPS, room=60):
    return pl.pallas_call(
        kernel,
        name=name,
        grid=(steps,),
        in_specs=ins,
        out_specs=outs,
        scratch_shapes=scratch,
        out_shape=out_shapes,
        compiler_params=pltpu.CompilerParams(vmem_limit_bytes=room * 2**20),
        cost_estimate=COST,
    )


def half_rows(columns):
    return pl.BlockSpec((1, HALF, columns), lambda step: (step, 0, 0))


def blocks(value):
    return value.reshape(STEPS, ROWS, value.shape[1])


def four(value):
    return value.reshape(STEPS, 2, HALF, value.shape[1])


def per_device(
    tokens, w_qkv, b_qkv, w_out, w_up, b_up, w_down, out_bias,
    ln1_gain, ln1_shift, ln2_gain, ln2_shift, cotangent,
):
    model = w_up.shape[0]
    feed_here = w_up.shape[1]
    wide = 3 * HEAD
    w_qkv = w_qkv.transpose(1, 2, 0).reshape(wide, model)
    w_out = w_out.reshape(HEAD, model)
    vecs = jnp.stack([ln1_gain, ln1_shift, ln2_gain, ln2_shift]).astype(F32)
    cosine, sine = rotary_tables()
    own_sum = jnp.sum(cotangent.astype(F32), axis=0)[None, :]

    held = copies(cotangent, 8)
    mine = trade_chips(copies(tokens, 8))
    weights_in = [swap_core(w) for w in (w_out, w_down, w_qkv, w_up)]
    held, vecs, b_qkv, b_up, own_sum, mine, *weights_in = lax.optimization_barrier(
        (held, vecs, b_qkv.astype(F32), b_up.astype(F32)[None, :], own_sum, mine)
        + tuple(weights_in)
    )
    w_out_in, w_down_in, w_qkv_in, w_up_in = weights_in
    other = swap_core(mine)
    grad_mine = trade_chips(held)

    halves = shape((STEPS, HALF, feed_here), LOW)
    (
        stats, queries, keys, values, active, active_send, slope, context, context_send, mass,
    ) = launch(
        forward_kernel,
        "forward",
        [
            LEFT, LEFT, whole((4, model)), whole((wide, model)), whole((1, wide)),
            whole((model, feed_here)), whole((1, feed_here)), by_rows(128), by_rows(128),
        ],
        [
            by_rows(128), whole((LEN, HEAD)),
            whole((LEN, HEAD)), whole((LEN, HEAD)), by_rows(feed_here), half_rows(feed_here),
            by_rows(feed_here), by_rows(HEAD), half_rows(HEAD), MASS,
        ],
        [
            left((LEN, 128), F32),
            shape((LEN, HEAD), LOW), shape((LEN, HEAD), LOW), shape((LEN, HEAD), LOW),
            left((LEN, feed_here), LOW), halves, left((LEN, feed_here), F32),
            shape((LEN, HEAD), LOW), shape((STEPS, HALF, HEAD), LOW),
            shape((STEPS, 1, ROWS), F32),
        ],
        [
            pltpu.VMEM((STEPS, ROWS, model), LOW), pltpu.VMEM((ROWS, model), LOW),
            pltpu.VMEM((ROWS, model), LOW), arrivals(STEPS), arrivals(STEPS),
        ],
    )(mine, other, vecs, w_qkv, b_qkv, w_up, b_up, cosine, sine)
    active_in = swap_core(active_send)
    context_in = swap_core(context_send)

    mixed = launch(
        mix_kernel,
        "mix",
        [LEFT] * 4 + [whole((HEAD, model)), whole((feed_here, model))] * 2,
        pl.BlockSpec((2, HALF, model), lambda step: (step, 0, 0)),
        left((STEPS, HALF, model), LOW),
        [pltpu.VMEM((STEPS, HALF, HEAD), LOW), pltpu.VMEM((STEPS, HALF, feed_here), LOW)] * 2
        + [arrivals(1)] * 4,
        steps=4,
    )(four(context), four(active), context_in, active_in, w_out, w_down, w_out_in, w_down_in)

    grad_mine, mixed = lax.optimization_barrier((grad_mine, mixed))
    grad_other = swap_core(grad_mine)
    branch = trade_chips(mixed)

    grad_hidden, hidden_send, grad_context, *feed, grad_out = launch(
        feed_back_kernel,
        "feed_back",
        [
            *[LEFT] * 7, whole((4, model)),
            by_rows(HEAD), whole((feed_here, model)), whole((HEAD, model)),
        ],
        [by_rows(feed_here), half_rows(feed_here), by_rows(HEAD)]
        + [whole((528, 256))] * 4 + [whole((HEAD, model))],
        [shape((LEN, feed_here), LOW), halves, shape((LEN, HEAD), LOW)]
        + [shape((528, 256), LOW)] * 4 + [shape((HEAD, model), LOW)],
        [
            pltpu.VMEM((STEPS, ROWS, model), LOW), pltpu.VMEM((STEPS, ROWS, feed_here), LOW),
            pltpu.VMEM((STEPS, ROWS, feed_here), F32), pltpu.VMEM((STEPS, ROWS, model), LOW),
            pltpu.VMEM((STEPS, ROWS, 128), F32), pltpu.VMEM((ROWS, model), LOW),
            pltpu.VMEM((feed_here, model), F32), pltpu.VMEM((feed_here, model), F32),
            pltpu.VMEM((HEAD, model), F32), pltpu.VMEM((1, feed_here), F32),
        ]
        + [arrivals(STEPS)] * 7,
    )(
        grad_mine, grad_other, blocks(active), blocks(slope), mine, other, blocks(stats), vecs,
        context, w_down, w_out,
    )
    hidden_in = swap_core(hidden_send)
    feed_moved = [move_x(feed[distance], distance) for distance in range(1, 4)]

    grad_projected, projected_send, *head, sums = launch(
        attend_back_kernel,
        "attend_back",
        [
            whole((LEN, HEAD)), whole((LEN, HEAD)), whole((LEN, HEAD)), by_rows(HEAD), MASS,
            *[LEFT] * 8, whole((4, model)), whole((1, model)), whole((HEAD, model)),
        ],
        [whole((LEN, wide)), whole((STEPS, HALF, wide))] + [whole((272, 256))] * 4
        + [whole((5, model))],
        [shape((LEN, wide), LOW), shape((STEPS, HALF, wide), LOW)]
        + [shape((272, 256), LOW)] * 4 + [shape((5, model), F32)],
        [pltpu.VMEM((LEN, HEAD), F32)] * 3
        + [
            pltpu.VMEM((wide, model), F32), pltpu.VMEM((wide + feed_here, model), F32),
            pltpu.VMEM((ROWS, model), LOW), pltpu.VMEM((ROWS, model), LOW),
            pltpu.VMEM((LEN, 128), F32), pltpu.VMEM((LEN, 128), F32),
            pltpu.VMEM((LEN, feed_here), LOW), pltpu.VMEM((LEN, 128), F32),
            pltpu.VMEM((STEPS, ROWS, model), LOW), pltpu.VMEM((wide, model), LOW),
            pltpu.VMEM((model, feed_here), LOW),
        ]
        + [pltpu.SemaphoreType.DMA] * 8,
    )(
        queries, keys, values, grad_context, mass, cosine, sine, grad_hidden, stats, mine, other,
        w_qkv, w_up, vecs, own_sum, grad_out,
    )
    sums_in = swap_core(sums)
    head_moved = [move_x(head[distance], distance) for distance in range(1, 4)]
    grad_projected, projected_send, branch, hidden_in, *feed_moved = lax.optimization_barrier(
        (grad_projected, projected_send, branch, hidden_in, *feed_moved)
    )
    projected_in = swap_core(projected_send)

    both = launch(
        input_back_kernel,
        "input_back",
        [LEFT] * 4 + [whole((4, model))] + [whole((wide, model)), whole((model, feed_here))] * 2,
        pl.BlockSpec((2, HALF, model), lambda step: (step, 0, 0)),
        left((STEPS, HALF, model), LOW),
        [pltpu.VMEM((STEPS, HALF, wide), LOW), pltpu.VMEM((STEPS, HALF, feed_here), LOW)] * 2
        + [arrivals(1)] * 4,
        steps=4,
    )(
        four(grad_projected), four(grad_hidden), projected_in, hidden_in, vecs,
        w_qkv, w_up, w_qkv_in, w_up_in,
    )
    both, sums, sums_in, *head_moved = lax.optimization_barrier(
        (both, sums, sums_in, *head_moved)
    )
    half = jnp.concatenate([add_four(feed[0], feed_moved), add_four(head[0], head_moved)], axis=0)
    other_half = lax.ppermute(half, "dp", Z_PAIR)
    scaled = trade_y(both.reshape(4, 2 * HALF, model))
    small = sums + sums_in
    near = lax.ppermute(small, "tensor", Z_NEAR)
    far = lax.ppermute(small, "dp", Z_PAIR)
    both_z = [(d * 16 + t, (d ^ 1) * 16 + (t ^ 2)) for d in range(8) for t in range(16)]
    across = lax.ppermute(small, ("dp", "tensor"), both_z)
    other_half, small = lax.optimization_barrier((other_half, (small + near) + (far + across)))
    small = sum_four(small, move_x)
    parts = spread_x(add_low(half, other_half))
    small = sum_four(small, move_y)

    layer_out = pl.pallas_call(
        finish_out_kernel,
        name="finish_out",
        out_shape=shape(tokens.shape, LOW),
        cost_estimate=COST,
    )(branch, tokens, out_bias[None, :])
    grad_qkv, grad_qkv_bias, grad_out, grad_up, grad_up_bias, grad_down = pl.pallas_call(
        finish_grads_kernel,
        name="finish_grads",
        out_shape=[
            shape((wide, model), F32), shape((1, wide), F32), shape((HEAD, model), F32),
            shape((model, feed_here), F32), shape((1, feed_here), F32),
            shape((feed_here, model), F32),
        ],
        cost_estimate=COST,
    )(*parts)
    scaled, layer_out, small = lax.optimization_barrier((scaled, layer_out, small))
    keep, send = pl.pallas_call(
        fold_kernel,
        name="fold",
        out_shape=[
            shape((HALF, model), F32), shape((HALF, model), LOW),
        ],
        cost_estimate=COST,
    )(scaled)
    received = lax.ppermute(send, "tensor", Z_NEAR)
    input_grad = pl.pallas_call(
        finish_back_kernel,
        name="finish_back",
        grid=(1,),
        in_specs=[
            whole((HALF, model)), whole((HALF, model)), whole(tokens.shape),
            whole(tokens.shape),
        ],
        out_specs=whole(tokens.shape),
        out_shape=shape(tokens.shape, LOW),
        cost_estimate=COST,
    )(keep, received, tokens, cotangent)

    return (
        layer_out,
        input_grad,
        grad_qkv.reshape(1, wide, model).transpose(2, 0, 1),
        grad_qkv_bias,
        grad_out.reshape(1, HEAD, model),
        grad_up,
        grad_up_bias[0],
        grad_down,
        small[4],
        small[0],
        small[1],
        small[2],
        small[3],
    )


def solution(mesh):
    placed = (
        P(("dp", "tensor"), None),
        P(None, "tensor", None),
        P("tensor", None),
        P("tensor", None, None),
        P(None, "tensor"),
        P("tensor"),
        P("tensor", None),
        P(),
        P(),
        P(),
        P(),
        P(),
        P(("dp", "tensor"), None),
    )
    return jax.shard_map(
        per_device,
        mesh=mesh,
        in_specs=placed,
        out_specs=(
            P(("dp", "tensor"), None),
            P(("dp", "tensor"), None),
            P(None, "tensor", None),
            P("tensor", None),
            P("tensor", None, None),
            P(None, "tensor"),
            P("tensor"),
            P("tensor", None),
            P(),
            P(),
            P(),
            P(),
            P(),
        ),
        check_vma=False,
    )
```

```python
from functools import partial

import jax
import jax.numpy as jnp
import numpy as np
from jax import lax
from jax.experimental import pallas as pl
from jax.experimental.pallas import tpu as pltpu
from jax.sharding import PartitionSpec as P

ROT = 16
LEN = 2048
EPS = 1e-05
HEAD = 64
ROWS = 256
STEPS = LEN // ROWS
HALF = ROWS // 2
SCALE = HEAD ** (-0.5)

SAME_CORE = [[c + 2 * i for i in range(8)] for c in range(2)]
SAME_Y = [[c + 4 * i for i in range(4)] for c in range(4)]
PAIR = [(i, i ^ 1) for i in range(16)]
Z_NEAR = [(i, i ^ 2) for i in range(16)]
Z_PAIR = [(i, i ^ 1) for i in range(8)]

F32 = jnp.float32
LOW = jnp.bfloat16


def swap_core(value):
    return lax.ppermute(value, "tensor", PAIR)


def trade_chips(blocks):
    return lax.all_to_all(blocks, "tensor", 0, 0, axis_index_groups=SAME_CORE, tiled=True)


def trade_y(blocks):
    return lax.all_to_all(blocks, "tensor", 0, 0, axis_index_groups=SAME_Y, tiled=True)


def copies(block, count):
    return jnp.broadcast_to(block[None], (count,) + block.shape)


def move_x(value, distance):
    pairs = [(i, (i // 2 + distance) % 4 * 2 + i % 2) for i in range(8)]
    return lax.ppermute(value, "dp", pairs)


def add_four(own, moved):
    total = own.astype(F32)
    for part in moved:
        total = total + part.astype(F32)
    return total.astype(LOW)


def add_low(left, right):
    return (left.astype(F32) + right.astype(F32)).astype(LOW)


def sum_four(rows, move):
    return (rows + move(rows, 2)) + (move(rows, 1) + move(rows, 3))


def move_y(value, distance):
    pairs = [(i, (i // 4 + distance) % 4 * 4 + i % 4) for i in range(16)]
    return lax.ppermute(value, "tensor", pairs)


def spread_x(low):
    return [low] + [move_x(low, distance) for distance in range(1, 4)]


def normalize(values):
    center = values - jnp.mean(values, axis=-1, keepdims=True)
    inverse = lax.rsqrt(jnp.mean(center * center, axis=-1, keepdims=True) + EPS)
    return (center * inverse, inverse)


def norm_back(scaled, normalized, inverse):
    centered = scaled - jnp.mean(scaled, axis=-1, keepdims=True)
    return inverse * (centered - normalized * jnp.mean(scaled * normalized, axis=-1, keepdims=True))


def rotary_tables():
    lane = np.arange(2 * HEAD) % HEAD
    half = ROT // 2
    inverse = np.float32(10000.0) ** (-2.0 * (lane % half).astype(np.float32) / np.float32(ROT))
    inverse = np.where(lane < ROT, inverse, 0.0).astype(np.float32)
    angles = np.arange(LEN, dtype=np.float32)[:, None] * inverse[None, :]
    sign = np.where(lane < half, -1.0, 1.0).astype(np.float32)
    return np.cos(angles).astype(np.float32), (np.sin(angles) * sign).astype(np.float32)


def turn(values, cosine, sine):
    lane = lax.broadcasted_iota(jnp.int32, values.shape, 1) % HEAD
    partner = jnp.where(
        lane < ROT // 2,
        pltpu.roll(values, 2 * HEAD - ROT // 2, 1),
        pltpu.roll(values, ROT // 2, 1),
    )
    return values * cosine + partner * sine


def dot(left, right, left_axis=1, right_axis=0):
    return lax.dot_general(
        left,
        right,
        (((left_axis,), (right_axis,)), ((), ())),
        preferred_element_type=F32,
    )


def core_here():
    return lax.axis_index("tensor") % 2


def stream(steps, each, moves):
    step = pl.program_id(0)

    @pl.when(step == 0)
    def _():
        for place in range(steps // each):
            for move in moves:
                move(place).start()

    @pl.when(step % each == 0)
    def _():
        for move in moves:
            move(step // each).wait()


def fetch(source, target, done):
    def move(place):
        return pltpu.make_async_copy(source(place), target(place), done.at[place])

    return move


def fetch_rows(source, target, done, each):
    return fetch(
        lambda place: source.at[pl.ds(place * each, each)],
        lambda place: target.at[pl.ds(place * each, each)],
        done,
    )


def fetch_parity(source, target, done, each):
    core = core_here()
    return fetch(
        lambda place: source.at[pl.ds(place * each, each), core],
        lambda place: target.at[pl.ds(place * each, each)],
        done,
    )


def fetch_joined(source, target, done, each, core):
    start = pl.multiple_of(core * HALF, HALF)
    return fetch(
        lambda place: source.at[pl.ds(place * each, each)],
        lambda place: target.at[pl.ds(place * each, each), pl.ds(start, HALF)],
        done,
    )


def send_rows(block, send):
    core = core_here()
    send[0] = block[pl.ds(pl.multiple_of((1 - core) * HALF, HALF), HALF), :]


def x_here():
    return lax.axis_index("dp") // 2


def renormalize(rows, stats):
    return (rows.astype(F32) - stats[:, 0:1]) * stats[:, 1:2]


def row_sum(values):
    return jnp.sum(values, axis=0, keepdims=True)


def forward_kernel(
    mine, other, vecs, w_qkv, b_qkv, w_up, b_up, cosine, sine,
    stats, queries, keys, values, active, active_send, slope,
    context, context_send, mass, rows, first, second, mine_done, other_done,
):
    core = core_here()
    stream(
        STEPS,
        2,
        [
            fetch_joined(mine, rows, mine_done, 2, core),
            fetch_joined(other, rows, other_done, 2, 1 - core),
        ],
    )
    step = pl.program_id(0)
    for part in range(0, ROWS, 32):
        span = slice(part, part + 32)
        here = rows[step, span, :].astype(F32)
        mean = jnp.mean(here, axis=-1, keepdims=True)
        center = here - mean
        inverse = lax.rsqrt(jnp.mean(center * center, axis=-1, keepdims=True) + EPS)
        normalized = center * inverse
        lane = lax.broadcasted_iota(jnp.int32, (32, 128), 1)
        stats[span, :] = jnp.where(lane == 0, mean, inverse)
        first[span, :] = (normalized * vecs[0:1, :] + vecs[1:2, :]).astype(LOW)
        second[span, :] = (normalized * vecs[2:3, :] + vecs[3:4, :]).astype(LOW)
    projected = dot(first[...], w_qkv[...], 1, 1) + b_qkv[...]
    turned = turn(projected[:, : 2 * HEAD], cosine[...], sine[...])
    here = pl.ds(pl.multiple_of(step * ROWS, ROWS), ROWS)
    queries[here, :] = turned[:, :HEAD].astype(LOW) * SCALE
    keys[here, :] = turned[:, HEAD:].astype(LOW)
    values[here, :] = projected[:, 2 * HEAD :].astype(LOW)
    for part in range(0, ROWS, 64):
        span = slice(part, part + 64)
        hidden = dot(second[span, :], w_up[...]) + b_up[...]
        share = 0.5 * (1.0 + lax.erf(hidden * (0.5**0.5)))
        active[span, :] = (hidden * share).astype(LOW)
        bell = jnp.exp(-0.5 * hidden * hidden) * ((2.0 * np.pi) ** -0.5)
        slope[span, :] = share + hidden * bell
    send_rows(active, active_send)

    place = lax.broadcasted_iota(jnp.int32, (ROWS, ROWS), 0)
    query = lax.broadcasted_iota(jnp.int32, (ROWS, ROWS), 1)
    seen = place <= query

    def block(index):
        low, high = index * ROWS, (index + 1) * ROWS
        asked = queries[low:high, :]
        near = jnp.where(seen, dot(keys[low:high, :], asked, 1, 1), -1e30)
        top = jnp.max(near, axis=0, keepdims=True)
        if index:
            far = dot(keys[:low, :], asked, 1, 1)
            top = jnp.maximum(top, jnp.max(far, axis=0, keepdims=True))
            far = jnp.exp(far - top)
        near = jnp.exp(near - top)
        total = row_sum(near)
        if index:
            total = total + row_sum(far)
        scale = 1.0 / total
        mass[0] = top + jnp.log(total)
        found = dot(values[low:high, :], (near * scale).astype(LOW), 0, 0)
        if index:
            found = found + dot(values[:low, :], (far * scale).astype(LOW), 0, 0)
        context[...] = found.T.astype(LOW)

    for index in range(STEPS):
        pl.when(step == index)(partial(block, index))
    send_rows(context, context_send)


def flat(block):
    return block.reshape(ROWS, block.shape[-1])


def mix_kernel(
    context, active, context_in, active_in, w_out, w_down, w_out_in, w_down_in, result,
    context_rows, active_rows, context_other, active_other, *done,
):
    stream(
        STEPS // 2,
        STEPS // 2,
        [
            fetch_parity(context, context_rows, done[0], STEPS),
            fetch_parity(active, active_rows, done[1], STEPS),
            fetch_rows(context_in, context_other, done[2], STEPS),
            fetch_rows(active_in, active_other, done[3], STEPS),
        ],
    )
    here = pl.ds(pl.program_id(0) * 2, 2)
    mixed = dot(flat(context_rows[here]), w_out[...])
    mixed = mixed + dot(flat(active_rows[here]), w_down[...])
    mixed = mixed + dot(flat(context_other[here]), w_out_in[...])
    mixed = mixed + dot(flat(active_other[here]), w_down_in[...])
    result[...] = mixed.astype(LOW).reshape(2, HALF, mixed.shape[1])


def feed_back_kernel(
    mine, other, active, slope, tokens_mine, tokens_other, stats, vecs, context, w_down, w_out,
    grad_hidden, hidden_send, grad_context, feed_0, feed_1, feed_2, feed_3, grad_out,
    rows, active_rows, slope_rows, token_rows, stats_rows, second, up_sum, down_sum, out_sum,
    bias_sum, *done,
):
    step = pl.program_id(0)
    core = core_here()
    stream(
        STEPS,
        2,
        [
            fetch_joined(mine, rows, done[0], 2, core),
            fetch_joined(other, rows, done[1], 2, 1 - core),
            fetch_rows(active, active_rows, done[2], 2),
            fetch_rows(slope, slope_rows, done[3], 2),
            fetch_rows(stats, stats_rows, done[4], 2),
            fetch_joined(tokens_mine, token_rows, done[5], 2, core),
            fetch_joined(tokens_other, token_rows, done[6], 2, 1 - core),
        ],
    )

    @pl.when(step == 0)
    def _():
        up_sum[...] = jnp.zeros_like(up_sum)
        down_sum[...] = jnp.zeros_like(down_sum)
        out_sum[...] = jnp.zeros_like(out_sum)
        bias_sum[...] = jnp.zeros_like(bias_sum)

    grads = rows[step]
    hidden = (dot(grads, w_down[...], 1, 1) * slope_rows[step]).astype(LOW)
    grad_hidden[...] = hidden
    send_rows(grad_hidden, hidden_send)
    grad_context[...] = dot(grads, w_out[...], 1, 1).astype(LOW)
    down_sum[...] += dot(active_rows[step], grads, 0, 0)
    out_sum[...] += dot(context[...], grads, 0, 0)
    for part in range(0, ROWS, 32):
        span = slice(part, part + 32)
        normalized = renormalize(token_rows[step, span, :], stats_rows[step, span, :])
        second[span, :] = (normalized * vecs[2:3, :] + vecs[3:4, :]).astype(LOW)
    up_sum[...] += dot(hidden, second[...], 0, 0)
    bias_sum[...] += row_sum(hidden.astype(F32))

    @pl.when(step == STEPS - 1)
    def _():
        grad_out[...] = out_sum[...].astype(LOW)
        for slot, feed in enumerate((feed_0, feed_1, feed_2, feed_3)):
            span = quarter((x_here() + slot) % 4)
            feed[0:256, :] = up_sum[:, span].T.astype(LOW)
            feed[256:512, :] = down_sum[:, span].astype(LOW)
            feed[512:528, :] = jnp.broadcast_to(bias_sum[...], (16, 256)).astype(LOW)


def quarter(part):
    return pl.ds(pl.multiple_of(part * 256, 256), 256)


def attend_back_kernel(
    queries, keys, values, grad_context, mass, cosine, sine, grad_hidden, stats, mine, other,
    w_qkv, w_up, vecs, own_sum, grad_out,
    grad_projected, projected_send, head_0, head_1, head_2, head_3, sums,
    query_sum, key_sum, value_sum, qkv_sum, moments, first, normal,
    cosine_rows, sine_rows, hidden_rows, stats_rows, token_rows, qkv_rows, up_rows, *done,
):
    wide = 3 * HEAD

    def later():
        pairs = [
            (cosine, cosine_rows), (sine, sine_rows), (grad_hidden, hidden_rows),
            (stats, stats_rows), (w_qkv, qkv_rows), (w_up, up_rows),
        ]
        for source, core in ((mine, core_here()), (other, 1 - core_here())):
            start = pl.multiple_of(core * HALF, HALF)
            pairs.append((source, token_rows.at[:, pl.ds(start, HALF)]))
        return [pltpu.make_async_copy(*pair, mark) for pair, mark in zip(pairs, done)]

    @pl.when(pl.program_id(0) == 0)
    def _():
        for copy in later():
            copy.start()

    place = lax.broadcasted_iota(jnp.int32, (ROWS, ROWS), 0)
    query = lax.broadcasted_iota(jnp.int32, (ROWS, ROWS), 1)
    seen = place <= query

    @pl.when(pl.program_id(0) == 0)
    def _():
        key_sum[...] = jnp.zeros_like(key_sum)
        value_sum[...] = jnp.zeros_like(value_sum)

    def block(index):
        low, high = index * ROWS, (index + 1) * ROWS
        asked = queries[low:high, :]
        grads = grad_context[...]
        spans = [slice(low, high)] + ([slice(0, low)] if index else [])
        weights, pulls = [], []
        inner = 0.0
        for number, span in enumerate(spans):
            scores = dot(keys[span, :], asked, 1, 1)
            if number == 0:
                scores = jnp.where(seen, scores, -1e30)
            weight = jnp.exp(scores - mass[0])
            pull = dot(values[span, :], grads, 1, 1)
            inner = inner + row_sum(weight * pull)
            weights.append(weight)
            pulls.append(pull)
        asked_grad = 0.0
        for span, weight, pull in zip(spans, weights, pulls):
            value_sum[span, :] += dot(weight.astype(LOW), grads)
            scores_grad = (weight * (pull - inner)).astype(LOW)
            key_sum[span, :] += dot(scores_grad, asked)
            asked_grad = asked_grad + dot(keys[span, :], scores_grad, 0, 0)
        query_sum[low:high, :] = asked_grad.T * SCALE

    for index in range(STEPS):
        pl.when(pl.program_id(0) == index)(partial(block, index))

    @pl.when(pl.program_id(0) == STEPS - 1)
    def _():
        for copy in later():
            copy.wait()
        for index in range(STEPS):
            span = slice(index * ROWS, (index + 1) * ROWS)
            both = jnp.concatenate([query_sum[span, :], key_sum[span, :]], axis=1)
            turned = turn(both, cosine_rows[span, :], -sine_rows[span, :])
            grad_projected[span, : 2 * HEAD] = turned.astype(LOW)
            grad_projected[span, 2 * HEAD :] = value_sum[span, :].astype(LOW)
            place = index * ROWS + (1 - core_here()) * HALF
            projected_send[index] = grad_projected[pl.ds(pl.multiple_of(place, HALF), HALF), :]
        hidden_bias, bias = 0.0, 0.0
        for index in range(STEPS):
            span = slice(index * ROWS, (index + 1) * ROWS)
            for part in range(0, ROWS, 32):
                rows = slice(part, part + 32)
                place = slice(index * ROWS + part, index * ROWS + part + 32)
                normalized = renormalize(token_rows[index, rows, :], stats_rows[place, :])
                normal[rows, :] = normalized.astype(LOW)
                first[rows, :] = (normalized * vecs[0:1, :] + vecs[1:2, :]).astype(LOW)
            grads = grad_projected[span, :]
            hidden = hidden_rows[span, :]
            here = normal[...]
            added = dot(grads, first[...], 0, 0), dot(grads, here, 0, 0), dot(hidden, here, 0, 0)
            if index:
                qkv_sum[...] += added[0]
                moments[0:wide, :] += added[1]
                moments[wide:, :] += added[2]
            else:
                qkv_sum[...] = added[0]
                moments[0:wide, :] = added[1]
                moments[wide:, :] = added[2]
            bias = bias + row_sum(grads.astype(F32))
            hidden_bias = hidden_bias + row_sum(hidden.astype(F32))
        for slot, head in enumerate((head_0, head_1, head_2, head_3)):
            span = quarter((x_here() + slot) % 4)
            head[0:wide, :] = qkv_sum[:, span].astype(LOW)
            head[wide:256, :] = grad_out[:, span]
            head[256:272, :wide] = jnp.broadcast_to(bias, (16, wide)).astype(LOW)
            head[256:272, wide:] = jnp.zeros((16, 256 - wide), LOW)
        sums[0:1, :] = row_sum(moments[0:wide, :] * qkv_rows[...].astype(F32))
        sums[1:2, :] = dot_full(bias, qkv_rows[...], 0)
        sums[2:3, :] = row_sum(moments[wide:, :] * up_rows[...].astype(F32).T)
        sums[3:4, :] = dot_full(hidden_bias, up_rows[...], 1)
        sums[4:5, :] = own_sum[...]


def input_back_kernel(
    projected, hidden, projected_in, hidden_in, vecs, w_qkv, w_up, w_qkv_in, w_up_in,
    result, projected_rows, hidden_rows, projected_other, hidden_other, *done,
):
    stream(
        STEPS // 2,
        STEPS // 2,
        [
            fetch_parity(projected, projected_rows, done[0], STEPS),
            fetch_parity(hidden, hidden_rows, done[1], STEPS),
            fetch_rows(projected_in, projected_other, done[2], STEPS),
            fetch_rows(hidden_in, hidden_other, done[3], STEPS),
        ],
    )
    here = pl.ds(pl.program_id(0) * 2, 2)
    one = dot(flat(projected_rows[here]), w_qkv[...])
    one = one + dot(flat(projected_other[here]), w_qkv_in[...])
    two = dot(flat(hidden_rows[here]), w_up[...], 1, 1)
    two = two + dot(flat(hidden_other[here]), w_up_in[...], 1, 1)
    weighted = one * vecs[0:1, :] + two * vecs[2:3, :]
    result[...] = weighted.astype(LOW).reshape(2, HALF, weighted.shape[1])


def dot_full(left, right, right_axis):
    return lax.dot_general(
        left,
        right.astype(F32),
        (((1,), (right_axis,)), ((), ())),
        precision=lax.Precision.HIGHEST,
        preferred_element_type=F32,
    )


def fold_kernel(parts, keep, send):
    own = lax.axis_index("tensor") // 2 % 2

    def total(start):
        span = pl.ds(pl.multiple_of(start, HALF), HALF)
        result = parts[0, span, :].astype(F32)
        for number in range(1, 4):
            result = result + parts[number, span, :].astype(F32)
        return result

    keep[...] = total(own * HALF)
    send[...] = total((1 - own) * HALF).astype(LOW)


def finish_grads_kernel(
    part_0, part_1, part_2, part_3,
    grad_qkv, grad_qkv_bias, grad_out, grad_up, grad_up_bias, grad_down,
):
    wide = 3 * HEAD
    for slot, part in enumerate((part_0, part_1, part_2, part_3)):
        span = quarter((x_here() + 4 - slot) % 4)
        grad_up[span, :] = part[0:256, :].astype(F32)
        grad_down[:, span] = part[256:512, :].astype(F32)
        grad_qkv[:, span] = part[528 : 528 + wide, :].astype(F32)
        grad_out[:, span] = part[528 + wide : 784, :].astype(F32)
    grad_up_bias[...] = part_0[512:513, :].astype(F32)
    grad_qkv_bias[...] = part_0[784:785, :wide].astype(F32)


def finish_out_kernel(parts, tokens, out_bias, layer_out):
    total = jnp.sum(parts[...].astype(F32), axis=0)
    layer_out[...] = (tokens[...].astype(F32) + total + out_bias[...].astype(F32)).astype(LOW)


def finish_back_kernel(keep, part, tokens, cotangent, input_grad):
    scaled = keep[...] + part[...].astype(F32)
    normalized, inverse = normalize(tokens[...].astype(F32))
    input_grad[...] = (
        cotangent[...].astype(F32) + norm_back(scaled, normalized, inverse)
    ).astype(LOW)


def arrivals(count):
    return pltpu.SemaphoreType.DMA((count,))


def whole(shape):
    return pl.BlockSpec(shape, lambda step: (0,) * len(shape))


def by_rows(columns):
    return pl.BlockSpec((ROWS, columns), lambda step: (step, 0))


LEFT = pl.BlockSpec(memory_space=pltpu.HBM)
MASS = pl.BlockSpec((1, 1, ROWS), lambda step: (step, 0, 0))


def shape(dims, kind):
    return jax.ShapeDtypeStruct(dims, kind)


COST = pl.CostEstimate(flops=1, bytes_accessed=1, transcendentals=0)


def left(dims, kind):
    return pltpu.HBM(dims, kind)


def launch(kernel, name, ins, outs, out_shapes, scratch, steps=STEPS, room=60):
    return pl.pallas_call(
        kernel,
        name=name,
        grid=(steps,),
        in_specs=ins,
        out_specs=outs,
        scratch_shapes=scratch,
        out_shape=out_shapes,
        compiler_params=pltpu.CompilerParams(vmem_limit_bytes=room * 2**20),
        cost_estimate=COST,
    )


def half_rows(columns):
    return pl.BlockSpec((1, HALF, columns), lambda step: (step, 0, 0))


def blocks(value):
    return value.reshape(STEPS, ROWS, value.shape[1])


def four(value):
    return value.reshape(STEPS, 2, HALF, value.shape[1])


def per_device(
    tokens, w_qkv, b_qkv, w_out, w_up, b_up, w_down, out_bias,
    ln1_gain, ln1_shift, ln2_gain, ln2_shift, cotangent,
):
    model = w_up.shape[0]
    feed_here = w_up.shape[1]
    wide = 3 * HEAD
    w_qkv = w_qkv.transpose(1, 2, 0).reshape(wide, model)
    w_out = w_out.reshape(HEAD, model)
    vecs = jnp.stack([ln1_gain, ln1_shift, ln2_gain, ln2_shift]).astype(F32)
    cosine, sine = rotary_tables()
    own_sum = jnp.sum(cotangent.astype(F32), axis=0)[None, :]

    held = copies(cotangent, 8)
    mine = trade_chips(copies(tokens, 8))
    weights_in = [swap_core(w) for w in (w_out, w_down, w_qkv, w_up)]
    held, vecs, b_qkv, b_up, own_sum, mine, *weights_in = lax.optimization_barrier(
        (held, vecs, b_qkv.astype(F32), b_up.astype(F32)[None, :], own_sum, mine)
        + tuple(weights_in)
    )
    w_out_in, w_down_in, w_qkv_in, w_up_in = weights_in
    other = swap_core(mine)
    grad_mine = trade_chips(held)

    halves = shape((STEPS, HALF, feed_here), LOW)
    (
        stats, queries, keys, values, active, active_send, slope, context, context_send, mass,
    ) = launch(
        forward_kernel,
        "forward",
        [
            LEFT, LEFT, whole((4, model)), whole((wide, model)), whole((1, wide)),
            whole((model, feed_here)), whole((1, feed_here)), by_rows(128), by_rows(128),
        ],
        [
            by_rows(128), whole((LEN, HEAD)),
            whole((LEN, HEAD)), whole((LEN, HEAD)), by_rows(feed_here), half_rows(feed_here),
            by_rows(feed_here), by_rows(HEAD), half_rows(HEAD), MASS,
        ],
        [
            left((LEN, 128), F32),
            shape((LEN, HEAD), LOW), shape((LEN, HEAD), LOW), shape((LEN, HEAD), LOW),
            left((LEN, feed_here), LOW), halves, left((LEN, feed_here), F32),
            shape((LEN, HEAD), LOW), shape((STEPS, HALF, HEAD), LOW),
            shape((STEPS, 1, ROWS), F32),
        ],
        [
            pltpu.VMEM((STEPS, ROWS, model), LOW), pltpu.VMEM((ROWS, model), LOW),
            pltpu.VMEM((ROWS, model), LOW), arrivals(STEPS), arrivals(STEPS),
        ],
    )(mine, other, vecs, w_qkv, b_qkv, w_up, b_up, cosine, sine)
    active_in = swap_core(active_send)
    context_in = swap_core(context_send)

    mixed = launch(
        mix_kernel,
        "mix",
        [LEFT] * 4 + [whole((HEAD, model)), whole((feed_here, model))] * 2,
        pl.BlockSpec((2, HALF, model), lambda step: (step, 0, 0)),
        left((STEPS, HALF, model), LOW),
        [pltpu.VMEM((STEPS, HALF, HEAD), LOW), pltpu.VMEM((STEPS, HALF, feed_here), LOW)] * 2
        + [arrivals(1)] * 4,
        steps=4,
    )(four(context), four(active), context_in, active_in, w_out, w_down, w_out_in, w_down_in)

    grad_mine, mixed = lax.optimization_barrier((grad_mine, mixed))
    grad_other = swap_core(grad_mine)
    branch = trade_chips(mixed)

    grad_hidden, hidden_send, grad_context, *feed, grad_out = launch(
        feed_back_kernel,
        "feed_back",
        [
            *[LEFT] * 7, whole((4, model)),
            by_rows(HEAD), whole((feed_here, model)), whole((HEAD, model)),
        ],
        [by_rows(feed_here), half_rows(feed_here), by_rows(HEAD)]
        + [whole((528, 256))] * 4 + [whole((HEAD, model))],
        [shape((LEN, feed_here), LOW), halves, shape((LEN, HEAD), LOW)]
        + [shape((528, 256), LOW)] * 4 + [shape((HEAD, model), LOW)],
        [
            pltpu.VMEM((STEPS, ROWS, model), LOW), pltpu.VMEM((STEPS, ROWS, feed_here), LOW),
            pltpu.VMEM((STEPS, ROWS, feed_here), F32), pltpu.VMEM((STEPS, ROWS, model), LOW),
            pltpu.VMEM((STEPS, ROWS, 128), F32), pltpu.VMEM((ROWS, model), LOW),
            pltpu.VMEM((feed_here, model), F32), pltpu.VMEM((feed_here, model), F32),
            pltpu.VMEM((HEAD, model), F32), pltpu.VMEM((1, feed_here), F32),
        ]
        + [arrivals(STEPS)] * 7,
    )(
        grad_mine, grad_other, blocks(active), blocks(slope), mine, other, blocks(stats), vecs,
        context, w_down, w_out,
    )
    hidden_in = swap_core(hidden_send)
    feed_moved = [move_x(feed[distance], distance) for distance in range(1, 4)]

    grad_projected, projected_send, *head, sums = launch(
        attend_back_kernel,
        "attend_back",
        [
            whole((LEN, HEAD)), whole((LEN, HEAD)), whole((LEN, HEAD)), by_rows(HEAD), MASS,
            *[LEFT] * 8, whole((4, model)), whole((1, model)), whole((HEAD, model)),
        ],
        [whole((LEN, wide)), whole((STEPS, HALF, wide))] + [whole((272, 256))] * 4
        + [whole((5, model))],
        [shape((LEN, wide), LOW), shape((STEPS, HALF, wide), LOW)]
        + [shape((272, 256), LOW)] * 4 + [shape((5, model), F32)],
        [pltpu.VMEM((LEN, HEAD), F32)] * 3
        + [
            pltpu.VMEM((wide, model), F32), pltpu.VMEM((wide + feed_here, model), F32),
            pltpu.VMEM((ROWS, model), LOW), pltpu.VMEM((ROWS, model), LOW),
            pltpu.VMEM((LEN, 128), F32), pltpu.VMEM((LEN, 128), F32),
            pltpu.VMEM((LEN, feed_here), LOW), pltpu.VMEM((LEN, 128), F32),
            pltpu.VMEM((STEPS, ROWS, model), LOW), pltpu.VMEM((wide, model), LOW),
            pltpu.VMEM((model, feed_here), LOW),
        ]
        + [pltpu.SemaphoreType.DMA] * 8,
    )(
        queries, keys, values, grad_context, mass, cosine, sine, grad_hidden, stats, mine, other,
        w_qkv, w_up, vecs, own_sum, grad_out,
    )
    sums_in = swap_core(sums)
    head_moved = [move_x(head[distance], distance) for distance in range(1, 4)]
    grad_projected, projected_send, branch, hidden_in, *feed_moved = lax.optimization_barrier(
        (grad_projected, projected_send, branch, hidden_in, *feed_moved)
    )
    projected_in = swap_core(projected_send)

    both = launch(
        input_back_kernel,
        "input_back",
        [LEFT] * 4 + [whole((4, model))] + [whole((wide, model)), whole((model, feed_here))] * 2,
        pl.BlockSpec((2, HALF, model), lambda step: (step, 0, 0)),
        left((STEPS, HALF, model), LOW),
        [pltpu.VMEM((STEPS, HALF, wide), LOW), pltpu.VMEM((STEPS, HALF, feed_here), LOW)] * 2
        + [arrivals(1)] * 4,
        steps=4,
    )(
        four(grad_projected), four(grad_hidden), projected_in, hidden_in, vecs,
        w_qkv, w_up, w_qkv_in, w_up_in,
    )
    both, sums, sums_in, *head_moved = lax.optimization_barrier(
        (both, sums, sums_in, *head_moved)
    )
    half = jnp.concatenate([add_four(feed[0], feed_moved), add_four(head[0], head_moved)], axis=0)
    other_half = lax.ppermute(half, "dp", Z_PAIR)
    scaled = trade_y(both.reshape(4, 2 * HALF, model))
    small = sums + sums_in
    near = lax.ppermute(small, "tensor", Z_NEAR)
    far = lax.ppermute(small, "dp", Z_PAIR)
    both_z = [(d * 16 + t, (d ^ 1) * 16 + (t ^ 2)) for d in range(8) for t in range(16)]
    across = lax.ppermute(small, ("dp", "tensor"), both_z)
    layer_out = pl.pallas_call(
        finish_out_kernel,
        name="finish_out",
        out_shape=shape(tokens.shape, LOW),
        cost_estimate=COST,
    )(branch, tokens, out_bias[None, :])
    other_half, small, layer_out = lax.optimization_barrier(
        (other_half, (small + near) + (far + across), layer_out)
    )
    small = sum_four(small, move_x)
    parts = spread_x(add_low(half, other_half))


    grad_qkv, grad_qkv_bias, grad_out, grad_up, grad_up_bias, grad_down = pl.pallas_call(
        finish_grads_kernel,
        name="finish_grads",
        out_shape=[
            shape((wide, model), F32), shape((1, wide), F32), shape((HEAD, model), F32),
            shape((model, feed_here), F32), shape((1, feed_here), F32),
            shape((feed_here, model), F32),
        ],
        cost_estimate=COST,
    )(*parts)
    scaled, small = lax.optimization_barrier((scaled, small))
    keep, send = pl.pallas_call(
        fold_kernel,
        name="fold",
        out_shape=[
            shape((HALF, model), F32), shape((HALF, model), LOW),
        ],
        cost_estimate=COST,
    )(scaled)
    received = lax.ppermute(send, "tensor", Z_NEAR)
    small = sum_four(small, move_y)
    input_grad = pl.pallas_call(
        finish_back_kernel,
        name="finish_back",
        grid=(1,),
        in_specs=[
            whole((HALF, model)), whole((HALF, model)), whole(tokens.shape),
            whole(tokens.shape),
        ],
        out_specs=whole(tokens.shape),
        out_shape=shape(tokens.shape, LOW),
        cost_estimate=COST,
    )(keep, received, tokens, cotangent)

    return (
        layer_out,
        input_grad,
        grad_qkv.reshape(1, wide, model).transpose(2, 0, 1),
        grad_qkv_bias,
        grad_out.reshape(1, HEAD, model),
        grad_up,
        grad_up_bias[0],
        grad_down,
        small[4],
        small[0],
        small[1],
        small[2],
        small[3],
    )


def solution(mesh):
    placed = (
        P(("dp", "tensor"), None),
        P(None, "tensor", None),
        P("tensor", None),
        P("tensor", None, None),
        P(None, "tensor"),
        P("tensor"),
        P("tensor", None),
        P(),
        P(),
        P(),
        P(),
        P(),
        P(("dp", "tensor"), None),
    )
    return jax.shard_map(
        per_device,
        mesh=mesh,
        in_specs=placed,
        out_specs=(
            P(("dp", "tensor"), None),
            P(("dp", "tensor"), None),
            P(None, "tensor", None),
            P("tensor", None),
            P("tensor", None, None),
            P(None, "tensor"),
            P("tensor"),
            P("tensor", None),
            P(),
            P(),
            P(),
            P(),
            P(),
        ),
        check_vma=False,
    )
```
